128 devices in a mesh: row: 8 (over y, core), col: 16 (over x, z).
Axes of the slice: x: 4, y: 4, z: 4, core: 2. Of those that a mesh axis runs over, the one named last changes fastest.
Arguments:
- amp_tiles: bfloat16 [2048, 128, 128], P(('row', 'col')), may hold values from -6 to 6
- owner_col: int32 [2048, 1], P(('row', 'col')), may hold values from 0 to 15; in each aligned block of 16 rows (0 to 15, 16 to 31, ...) at most 2 rows name the same one
- local_pair: int32 [2048], P(('row', 'col')), may hold values from 0 to 31
- occ_pair: int32 [2048], P(('row', 'col')), may hold values from 0 to 15
- integrals: bfloat16 [65536, 8192], P('col', 'row'), may hold values from -0.046875 to 0.046875
Outputs:
- ladder: bfloat16 [2048, 8192], P('col', 'row')
The draws below stay inside these ranges and needn't reach their ends.
Inputs may be any that keep to these rules, and one draw needn't show every extreme that they name: `owner_col`: among the 16 tiles of one device, at most 2 name the same owner, and in every draw some device sends exactly 2 tiles to some owner.
All inputs are finite; a program needn't handle non-finite values.
Results may differ from the reference program's by a relative error of at most 0.018.
Values may be sent and summed in bfloat16 or wider, within the bound.
No kernel may reach another device: no remote copies, remote signals or barrier semaphores. Data moves between devices by JAX's collectives and lax.ppermute only.
A program may use at most 128 MiB of HBM per device.

```python
import math
import jax
import jax.numpy as jnp
import numpy as np
from jax import lax

TILE = 128
CAP = 2
TILES_DEV = 16
CD_DEV = 32
TILES = 2048
NCD = 512
NOT = 16
AB = 8192
N_COL = 16


def with_ends(drawn, stream_key, least, high):
    longest = drawn.shape.index(max(drawn.shape))
    spots = []
    for shift in (0, 1):
        where = [jax.random.randint(jax.random.fold_in(stream_key, axis), (), 0, length) for axis, length in enumerate(drawn.shape)]
        where[longest] = (where[longest] + shift) % drawn.shape[longest]
        spots.append(tuple(where))
    return drawn.at[spots[0]].set(least).at[spots[1]].set(high)


def block_scale(rng, extent, shards, low, top_value):
    gain = 1.0
    for axis_at, parts in shards:
        steps = jax.random.uniform(jax.random.fold_in(jax.random.fold_in(rng, 6), axis_at), (parts,), jnp.float32, low / len(shards), top_value / len(shards))
        gain = gain * jnp.repeat(jnp.exp(steps), extent[axis_at] // parts).reshape((-1,) + (1,) * (len(extent) - 1 - axis_at))
    return gain


def routed_block(rng, own, number, rows, number_of, top, reach, lean):
    order = jax.random.permutation(rng, number_of)
    heavy_load, ordinary = shares(number_of, rows * top, reach, lean, True), shares(number_of, rows * top, reach, lean, False)
    places = jnp.arange(number_of)

    def named(sizes, turn):
        used = int((sizes > 0).sum())
        fixed = max(1, used // 4)
        passed = fixed + (places - fixed + turn * (used - fixed)) % max(1, number_of - fixed)
        return jnp.zeros((number_of,), jnp.int32).at[order[jnp.where(places < fixed, places, passed)]].set(jnp.asarray(sizes, jnp.int32))

    sizes = jnp.where(number % 4 == 0, named(heavy_load, number // 4), named(ordinary, number - number // 4 - 1))
    mixed = jax.random.permutation(jax.random.fold_in(own, 3), number_of)
    donor, taker = mixed[0:number_of // 2 * 2:2], mixed[1:number_of // 2 * 2:2]
    margin = jnp.minimum(sizes[donor] - 1, reach - sizes[taker]) // 2
    margin = jnp.where((donor == order[0]) | (taker == order[0]) | (sizes[taker] == 0), 0, jnp.maximum(margin, 0))
    passed = jax.random.randint(jax.random.fold_in(own, 4), (number_of // 2,), 0, 1 << 20) % (margin + 1)
    sizes = sizes.at[donor].add(-passed).at[taker].add(passed)
    members = jnp.searchsorted(jnp.cumsum(sizes), jnp.arange(rows * top), side="right").astype(jnp.int32)
    grid = members.reshape(top, rows).T
    grid = grid[jax.random.permutation(jax.random.fold_in(own, 1), rows)]
    turn = jax.random.randint(jax.random.fold_in(own, 2), (rows, 1), 0, top)
    return jnp.take_along_axis(grid, (jnp.arange(top)[None, :] + turn) % top, axis=1)


def shares(count, total, limit, skew, full):
    loads = [(1 << 20) // math.isqrt(grade ** skew) + 1 for grade in range(1, count + 1)]
    largest = limit if full else min(limit, max(-(-total // count), total * loads[0] // sum(loads)))
    least = 1 if total - largest >= count - 1 else 0
    given, surplus = [largest] + [least] * (count - 1), total - largest - least * (count - 1)
    while surplus > 0:
        free = [i for i in range(1, count) if given[i] < largest] or [i for i in range(1, count) if given[i] < limit]
        mass, budget = sum([loads[i] for i in free]), surplus
        for i in free:
            more = min(limit - given[i], max(1, budget * loads[i] // mass), surplus)
            given[i] = given[i] + more
            surplus = surplus - more
    return np.array(given)


def normal_values(own_key, dims, spread, reach, pieces=(), kind=jnp.bfloat16):
    loudness = block_scale(own_key, dims, pieces, -0.22, 0.18) if pieces else 1.0
    drawn = jax.random.normal(own_key, dims, jnp.float32) * spread * loudness
    return jnp.minimum(jnp.maximum(drawn, -reach), reach).astype(kind)


def setup_inputs(seed: int = 0) -> dict:
    key_list = jax.random.split(jax.random.key(seed), 6)
    amp_tiles = normal_values(key_list[0], (TILES, TILE, TILE), 1.0, 6.0, ((0, 128),))
    owner_col_keys = jax.random.split(jax.random.fold_in(key_list[1], 1), TILES // TILES_DEV)
    owner_col_turns = jax.random.permutation(jax.random.fold_in(key_list[1], 3), TILES // TILES_DEV)
    owner_col = jax.vmap(lambda own, number: routed_block(jax.random.fold_in(key_list[1], 2), own, number, TILES_DEV, N_COL, 1, CAP, 2))(owner_col_keys, owner_col_turns).reshape((TILES, 1))
    local_pair = with_ends(jax.random.randint(key_list[2], (TILES,), 0, CD_DEV), jax.random.fold_in(key_list[2], 1), 0, CD_DEV - 1).astype(jnp.int32)
    occ_pair = with_ends(jax.random.randint(key_list[3], (TILES,), 0, NOT), jax.random.fold_in(key_list[3], 1), 0, NOT - 1).astype(jnp.int32)
    integrals = normal_values(key_list[4], (NCD * TILE, AB), (TILES * TILE // NOT) ** -0.5, 0.046875, ((0, 16), (1, 8)))
    return dict(amp_tiles=amp_tiles, owner_col=owner_col, local_pair=local_pair, occ_pair=occ_pair, integrals=integrals)


def reference(amp_tiles, owner_col, local_pair, occ_pair, integrals):
    owners = owner_col[:, 0]
    positions = NOT * CD_DEV
    tiles_wide = amp_tiles.astype(jnp.float32)
    blocks = integrals.reshape(N_COL, CD_DEV * TILE, AB)

    def one_owner(total, owner):
        target = jnp.where(owners == owner, occ_pair * CD_DEV + local_pair, positions).astype(jnp.int32)
        placed = jnp.zeros((positions, TILE, TILE), jnp.float32).at[target].add(tiles_wide, mode="drop")
        matrix = placed.astype(jnp.bfloat16).reshape(NOT, CD_DEV, TILE, TILE)
        matrix = matrix.transpose(0, 2, 1, 3).reshape(NOT * TILE, CD_DEV * TILE)
        block = lax.dynamic_index_in_dim(blocks, owner, 0, keepdims=False)
        partial_sum = jnp.dot(matrix, block, preferred_element_type=jnp.float32).astype(jnp.bfloat16)
        partial_sum = lax.optimization_barrier(partial_sum)
        return total + partial_sum.astype(jnp.float32), None

    start = jnp.zeros((NOT * TILE, AB), jnp.float32)
    total, unused = lax.scan(one_owner, start, jnp.arange(N_COL, dtype=jnp.int32))
    return total.astype(jnp.bfloat16)
```

```python
import jax
import jax.numpy as jnp
from jax import lax
from jax.experimental import pallas as pl
from jax.experimental.pallas import tpu as pltpu
from jax.sharding import PartitionSpec as P

SIDE = 128
CAP = 2
RING = 4
SLOTS = RING * CAP
HEAD = 16
MSG = SLOTS * SIDE + HEAD
PIECE = RING * MSG
OCC = RING * RING
DUMMY = OCC
UNROLL = 8

VMEM = pl.BlockSpec(memory_space=pltpu.VMEM)
SMEM = pl.BlockSpec(memory_space=pltpu.SMEM)
F32, BF16, I32 = jnp.float32, jnp.bfloat16, jnp.int32


def row_perm(step):
    return [(r, (r + 2 * step) % (2 * RING)) for r in range(2 * RING)]


CORE_PERM = [(r, r ^ 1) for r in range(2 * RING)]


def plane_perm(step, second):
    pairs = []
    for r in range(2 * RING):
        for x in range(RING):
            for z in range(RING):
                along_x = (r % 2 == 0) != second
                nx, nz = ((x + step) % RING, z) if along_x else (x, (z + step) % RING)
                pairs.append((r * OCC + x * RING + z, r * OCC + nx * RING + nz))
    return pairs


def send_first(v, step):
    return lax.ppermute(v, ("row", "col"), plane_perm(step, False))


def send_second(v, step):
    return lax.ppermute(v, ("row", "col"), plane_perm(step, True))


def send_y(v, step):
    return lax.ppermute(v, "row", row_perm(step))


def send_core(v):
    return lax.ppermute(v, "row", CORE_PERM)


def place():
    core = lax.rem(lax.axis_index("row"), 2)
    col = lax.axis_index("col")
    x, z = col // RING, lax.rem(col, RING)
    first = core == 0
    return first, jnp.where(first, x, z), jnp.where(first, z, x)


def relative(index, first, a, b):
    x, z = index >> 2, index & 3
    return (jnp.where(first, x, z) - a) & 3, (jnp.where(first, z, x) - b) & 3


def params(mib):
    return pltpu.CompilerParams(vmem_limit_bytes=mib * 2**20)


def header(occ_row, loc_row):
    rows = lax.broadcasted_iota(I32, (HEAD, SIDE), 0)
    occ = jnp.broadcast_to(occ_row, (HEAD, SIDE))
    loc = jnp.broadcast_to(loc_row, (HEAD, SIDE))
    return jnp.where(rows == 0, occ, jnp.where(rows == 1, loc, 0.0)).astype(BF16)


def sort_tiles_kernel(meta, tiles, *refs):
    outs, seen = refs[:RING], refs[RING]
    first, a, b = place()
    count = tiles.shape[0]
    for o in range(OCC):
        seen[o] = 0
    rows = lax.broadcasted_iota(I32, (8, SIDE), 0)
    lanes = lax.broadcasted_iota(I32, (8, SIDE), 1)
    occ_of = jnp.zeros((8, SIDE), F32)
    loc_of = jnp.zeros((8, SIDE), F32)
    for k in range(count):
        owner, loc, occ = meta[k], meta[count + k], meta[2 * count + k]
        rank = seen[owner]
        seen[owner] = rank + 1
        da, db = relative(owner, first, a, b)
        slot = db * CAP + rank
        here = (rows == da) & (lanes == slot)
        occ_of = jnp.where(here, (occ + 1).astype(F32), occ_of)
        loc_of = jnp.where(here, loc.astype(F32), loc_of)
        at = pl.ds(pl.multiple_of(slot * SIDE, SIDE), SIDE)
        for d in range(RING):

            @pl.when(da == d)
            def _(d=d, k=k, at=at):
                outs[d][at, :] = tiles[k]

    for d in range(RING):
        outs[d][SLOTS * SIDE :, :] = header(occ_of[d : d + 1], loc_of[d : d + 1])


def sort_tiles(meta, tiles):
    return pl.pallas_call(
        sort_tiles_kernel,
        in_specs=[SMEM, VMEM],
        out_specs=[VMEM] * RING,
        out_shape=[jax.ShapeDtypeStruct((MSG, SIDE), BF16)] * RING,
        scratch_shapes=[pltpu.SMEM((OCC,), I32)],
        compiler_params=params(8),
        name="sort_tiles",
    )(meta, tiles)


def turn_kernel(*refs):
    ins, outs = refs[:RING], refs[RING:]
    lanes = lax.broadcasted_iota(I32, (HEAD, SIDE), 1)
    heads = [r[SLOTS * SIDE :, :].astype(F32) for r in ins]
    for db in range(RING):
        head = jnp.zeros((HEAD, SIDE), F32)
        for da in range(RING):
            outs[db][da * CAP * SIDE : (da + 1) * CAP * SIDE, :] = ins[da][db * CAP * SIDE : (db + 1) * CAP * SIDE, :]
            turned = pltpu.roll(heads[da], ((da - db) * CAP) % SIDE, 1)
            head = jnp.where((lanes >= da * CAP) & (lanes < (da + 1) * CAP), turned, head)
        outs[db][SLOTS * SIDE :, :] = head.astype(BF16)


def turn(parts):
    return pl.pallas_call(
        turn_kernel,
        in_specs=[VMEM] * RING,
        out_specs=[VMEM] * RING,
        out_shape=[jax.ShapeDtypeStruct((MSG, SIDE), BF16)] * RING,
        compiler_params=params(8),
        name="turn",
    )(*parts)


def multiply_tiles(pieces, ints, acc, head_v, head_s, row_s, code_s, block_of, dummy):
    first, a, b = place()
    n = len(pieces)
    heads = []
    for piece in pieces:
        for m in range(RING):
            at = m * MSG + SLOTS * SIDE
            heads.append(piece[at : at + HEAD, :].astype(F32)[0:8].astype(I32))
    for i, h in enumerate(heads):
        occ = jnp.broadcast_to(h[0:1], (8, SIDE)) - 1
        loc = jnp.broadcast_to(h[1:2], (8, SIDE))
        da, db = relative(occ, first, a, b)
        wanted, block = block_of(da, db)
        head_v[i * 8 : (i + 1) * 8, :] = jnp.where((occ >= 0) & wanted, block * 32 + loc, -1)
    pltpu.sync_copy(head_v, head_s)
    for p, piece in enumerate(pieces):
        count = jnp.int32(0)
        for m in range(RING):
            for s in range(SLOTS):
                code = head_s[(p * RING + m) * 8, s]
                row_s[count] = m * MSG + s * SIDE
                code_s[count] = code
                count = count + (code >= 0).astype(I32)
        for i in range(UNROLL):
            row_s[count + i] = 0
            code_s[count + i] = dummy * 32

        def step(k):
            code = code_s[k]
            at = pl.multiple_of(row_s[k], 16)
            block = pl.multiple_of((code >> 5) * SIDE, SIDE)
            rows = pl.multiple_of((code & 31) * SIDE, SIDE)
            acc[pl.ds(block, SIDE), :] += jnp.dot(
                piece[pl.ds(at, SIDE), :], ints[pl.ds(rows, SIDE), :], preferred_element_type=F32
            )

        def body(i, carry):
            for u in range(UNROLL):
                step(i * UNROLL + u)
            return carry

        lax.fori_loop(0, (count + UNROLL - 1) // UNROLL, body, 0)


def list_scratch(n):
    return [
        pltpu.VMEM((n * RING * 8, SIDE), I32),
        pltpu.SMEM((n * RING * 8, SIDE), I32),
        pltpu.SMEM((RING * SLOTS + UNROLL,), I32),
        pltpu.SMEM((RING * SLOTS + UNROLL,), I32),
    ]


def kept(v):
    return pltpu.with_memory_space_constraint(v, pltpu.VMEM)


def all_blocks(da, db):
    return da >= 0, da * RING + db


def accumulate(total, ints, pieces, flops):
    n = len(pieces)
    width = ints.shape[1]
    old = [] if total is None else [total]

    def kernel(*refs):
        refs = refs[len(old) :]
        ints_ref, piece_refs, acc, scratch = refs[0], refs[1 : 1 + n], refs[1 + n], refs[2 + n :]
        if not old:
            acc[...] = jnp.zeros_like(acc)
        multiply_tiles(piece_refs, ints_ref, acc, *scratch, all_blocks, DUMMY)

    return pl.pallas_call(
        kernel,
        in_specs=[VMEM] * (len(old) + 1 + n),
        out_specs=VMEM,
        out_shape=pltpu.VMEM(((OCC + 1) * SIDE, width), F32),
        scratch_shapes=list_scratch(n),
        input_output_aliases={0: 0} if old else {},
        compiler_params=params(14),
        cost_estimate=pl.CostEstimate(flops=flops, bytes_accessed=2**22, transcendentals=0),
        name="accumulate",
    )(*[kept(v) for v in old], kept(ints), *pieces)


def finish(total, ints, pieces, blocks, block_of, outs, flops):
    n = len(pieces)
    width = ints.shape[1]
    size = len(blocks)

    def kernel(*refs):
        total_ref, ints_ref, piece_refs = refs[0], refs[1], refs[2 : 2 + n]
        out_refs = refs[2 + n : 2 + n + len(outs)]
        acc, scratch = refs[2 + n + len(outs)], refs[3 + n + len(outs) :]
        for i, (da, db) in enumerate(blocks):
            at = (da * RING + db) * SIDE
            acc[i * SIDE : (i + 1) * SIDE, :] = total_ref[at : at + SIDE, :]
        multiply_tiles(piece_refs, ints_ref, acc, *scratch, block_of, size)
        for ref, (start, many, dtype) in zip(out_refs, outs):
            ref[...] = acc[start * SIDE : (start + many) * SIDE, :].astype(dtype)

    return pl.pallas_call(
        kernel,
        in_specs=[VMEM] * (2 + n),
        out_specs=[VMEM] * len(outs),
        out_shape=[jax.ShapeDtypeStruct((many * SIDE, width), dtype) for _, many, dtype in outs],
        scratch_shapes=[pltpu.VMEM(((size + 1) * SIDE, width), F32)] + list_scratch(n),
        compiler_params=params(20),
        cost_estimate=pl.CostEstimate(flops=flops, bytes_accessed=2**22, transcendentals=0),
        name="finish",
    )(kept(total), kept(ints), *pieces)


def to_owner(meta, tiles):
    parts = sort_tiles(meta, tiles)
    parts = [parts[0]] + [send_first(parts[d], d) for d in range(1, RING)]
    parts = turn(parts)
    parts = [parts[0]] + [send_second(parts[d], d) for d in range(1, RING)]
    return jnp.concatenate(parts, axis=0)


def per_device(amp_tiles, owner_col, local_pair, occ_pair, integrals):
    meta = jnp.concatenate([owner_col[:, 0], local_pair, occ_pair])
    far_tiles, far_meta = send_y(amp_tiles, 2), send_y(meta, 2)

    own = to_owner(meta, amp_tiles)
    up, down = send_y(own, 1), send_y(own, -1)
    far = to_owner(far_meta, far_tiles)
    total = accumulate(None, integrals, [own, send_core(own)], 2**32)
    total = accumulate(total, integrals, [far, send_core(far)], 2**32)
    late = [up, down, send_core(up), send_core(down)]

    (far_a,) = finish(
        total, integrals, late, [(2, 1), (2, 2), (2, 3)], lambda da, db: ((da == 2) & (db > 0), db - 1), [(0, 3, BF16)], 2**31
    )
    got = [send_first(far_a, 2)]
    sides = finish(
        total,
        integrals,
        late,
        [(1, 1), (1, 2), (1, 3), (3, 1), (3, 2), (3, 3)],
        lambda da, db: (((da == 1) | (da == 3)) & (db > 0), jnp.where(da == 3, 2, -1) + db),
        [(0, 3, BF16), (3, 3, BF16)],
        2**31,
    )
    got += [send_first(sides[0], 1), send_first(sides[1], -1)]
    lasts = finish(
        total,
        integrals,
        late,
        [(1, 0), (2, 0), (3, 0)],
        lambda da, db: ((da > 0) & (db == 0), da - 1),
        [(i, 1, BF16) for i in range(3)],
        2**31,
    )
    got_last = [send_first(lasts[1], 2), send_first(lasts[0], 1), send_first(lasts[2], -1)]
    own_last, own_rest = finish(
        total,
        integrals,
        late,
        [(0, 0), (0, 1), (0, 2), (0, 3)],
        lambda da, db: (da == 0, db),
        [(0, 1, F32), (1, 3, F32)],
        2**31,
    )
    rest = own_rest + got[0].astype(F32) + got[1].astype(F32) + got[2].astype(F32)
    rest = rest.astype(BF16).reshape(3, SIDE, -1)
    ladder = own_last
    for g in got_last:
        ladder = ladder + g.astype(F32)
    for d in (2, 1, 3):
        ladder = ladder + send_second(rest[d - 1], d).astype(F32)
    return ladder.astype(BF16)


def solution(mesh):
    return jax.shard_map(
        per_device,
        mesh=mesh,
        in_specs=(
            P(("row", "col"), None, None),
            P(("row", "col"), None),
            P(("row", "col")),
            P(("row", "col")),
            P("col", "row"),
        ),
        out_specs=P("col", "row"),
        check_vma=False,
    )
```

```python
import jax
import jax.numpy as jnp
from jax import lax
from jax.experimental import pallas as pl
from jax.experimental.pallas import tpu as pltpu
from jax.sharding import PartitionSpec as P

SIDE = 128
CAP = 2
RING = 4
SLOTS = RING * CAP
HEAD = 16
MSG = SLOTS * SIDE + HEAD
PIECE = RING * MSG
OCC = RING * RING
DUMMY = OCC
UNROLL = 4
INFO = 32

VMEM = pl.BlockSpec(memory_space=pltpu.VMEM)
SMEM = pl.BlockSpec(memory_space=pltpu.SMEM)
ANY = pl.BlockSpec(memory_space=pl.ANY)
HBM = pl.BlockSpec(memory_space=pltpu.HBM)
F32, BF16, I32 = jnp.float32, jnp.bfloat16, jnp.int32


def row_perm(step):
    return [(r, (r + 2 * step) % (2 * RING)) for r in range(2 * RING)]


CORE_PERM = [(r, r ^ 1) for r in range(2 * RING)]


def plane_perm(step, second):
    pairs = []
    for r in range(2 * RING):
        for x in range(RING):
            for z in range(RING):
                along_x = (r % 2 == 0) != second
                nx, nz = ((x + step) % RING, z) if along_x else (x, (z + step) % RING)
                pairs.append((r * OCC + x * RING + z, r * OCC + nx * RING + nz))
    return pairs


def send_first(v, step):
    return lax.ppermute(v, ("row", "col"), plane_perm(step, False))


def send_second(v, step):
    return lax.ppermute(v, ("row", "col"), plane_perm(step, True))


def send_y(v, step):
    return lax.ppermute(v, "row", row_perm(step))


def send_core(v):
    return lax.ppermute(v, "row", CORE_PERM)


def place():
    core = lax.rem(lax.axis_index("row"), 2)
    col = lax.axis_index("col")
    x, z = col // RING, lax.rem(col, RING)
    first = core == 0
    return first, jnp.where(first, x, z), jnp.where(first, z, x)


def relative(index, first, a, b):
    x, z = index >> 2, index & 3
    return (jnp.where(first, x, z) - a) & 3, (jnp.where(first, z, x) - b) & 3


def params(mib):
    return pltpu.CompilerParams(vmem_limit_bytes=mib * 2**20)


def kept(v):
    return pltpu.with_memory_space_constraint(v, pltpu.VMEM)


def in_hbm(v):
    return pltpu.with_memory_space_constraint(v, pltpu.HBM)


def header(lines):
    rows = lax.broadcasted_iota(I32, (HEAD, SIDE), 0)
    head = jnp.zeros((HEAD, SIDE), F32)
    for i, line in enumerate(lines):
        head = jnp.where(rows == i, jnp.broadcast_to(line, (HEAD, SIDE)), head)
    return head.astype(BF16)


def sort_tiles_body(owner_of, loc_at, occ_at, tile_at, count, outs, seen):
    first, a, b = place()
    for o in range(OCC):
        seen[o] = 0
    rows = lax.broadcasted_iota(I32, (8, SIDE), 0)
    lanes = lax.broadcasted_iota(I32, (8, SIDE), 1)
    occ_of = jnp.zeros((8, SIDE), F32)
    loc_of = jnp.zeros((8, SIDE), F32)
    for k in range(count):
        owner = owner_of(k)
        rank = seen[owner]
        seen[owner] = rank + 1
        da, db = relative(owner, first, a, b)
        slot = db * CAP + rank
        here = (rows == da) & (lanes == slot)
        occ_of = jnp.where(here, (occ_at(k) + 1).astype(F32), occ_of)
        loc_of = jnp.where(here, loc_at(k).astype(F32), loc_of)
        at = pl.ds(pl.multiple_of(slot * SIDE, SIDE), SIDE)
        for d in range(RING):

            @pl.when(da == d)
            def _(d=d, k=k, at=at):
                outs[d][at, :] = tile_at(k)

    for d in range(RING):
        outs[d][SLOTS * SIDE :, :] = header([occ_of[d : d + 1], loc_of[d : d + 1]])


def sort_own(owner, loc, occ, tiles):
    count = tiles.shape[0]

    def kernel(owner_hbm, loc_hbm, occ_hbm, tiles_hbm, *refs):
        outs, raw, seen = refs[:RING], refs[RING], refs[RING + 1]
        owner_ref, loc_ref, occ_ref, sems = refs[RING + 2 :]
        pairs = [(owner_hbm, owner_ref), (loc_hbm, loc_ref), (occ_hbm, occ_ref)]
        pairs += [(tiles_hbm.at[k], raw.at[pl.ds(k * SIDE, SIDE), :]) for k in range(count)]
        copies = [pltpu.make_async_copy(src, dst, sems.at[i]) for i, (src, dst) in enumerate(pairs)]
        for copy in copies:
            copy.start()
        for copy in copies:
            copy.wait()
        sort_tiles_body(
            lambda k: owner_ref[k],
            lambda k: loc_ref[k],
            lambda k: occ_ref[k],
            lambda k: raw[k * SIDE : (k + 1) * SIDE, :],
            count,
            outs,
            seen,
        )
        lanes = lax.broadcasted_iota(I32, (8, SIDE), 1)
        rows = []
        for ref in (owner_ref, loc_ref, occ_ref):
            row = jnp.zeros((8, SIDE), F32)
            for k in range(count):
                row = jnp.where(lanes == k, ref[k].astype(F32), row)
            rows.append(row[0:1])
        raw[count * SIDE :, :] = header(rows)

    return pl.pallas_call(
        kernel,
        in_specs=[HBM] * 4,
        out_specs=[VMEM] * (RING + 1),
        out_shape=[pltpu.VMEM((MSG, SIDE), BF16)] * RING + [pltpu.VMEM((count * SIDE + HEAD, SIDE), BF16)],
        scratch_shapes=[pltpu.SMEM((OCC,), I32)]
        + [pltpu.SMEM((count,), I32)] * 3
        + [pltpu.SemaphoreType.DMA((3 + count,))],
        compiler_params=params(8),
        name="sort_own",
    )(*[in_hbm(v) for v in (owner, loc, occ, tiles)])


def sort_far(raw, after):
    count = (raw.shape[0] - HEAD) // SIDE

    def kernel(raw_ref, after_ref, *refs):
        outs, seen, head_v, head_s = refs[:RING], refs[RING], refs[RING + 1], refs[RING + 2]
        head_v[...] = raw_ref[count * SIDE :, :].astype(F32)[0:8].astype(I32)
        pltpu.sync_copy(head_v, head_s)
        sort_tiles_body(
            lambda k: head_s[0, k],
            lambda k: head_s[1, k],
            lambda k: head_s[2, k],
            lambda k: raw_ref[k * SIDE : (k + 1) * SIDE, :],
            count,
            outs,
            seen,
        )

    return pl.pallas_call(
        kernel,
        in_specs=[VMEM, ANY],
        out_specs=[VMEM] * RING,
        out_shape=[pltpu.VMEM((MSG, SIDE), BF16)] * RING,
        scratch_shapes=[pltpu.SMEM((OCC,), I32), pltpu.VMEM((8, SIDE), I32), pltpu.SMEM((8, SIDE), I32)],
        compiler_params=params(8),
        name="sort_far",
    )(kept(raw), after)


def turn_kernel(after, *refs):
    ins, outs = refs[:RING], refs[RING:]
    lanes = lax.broadcasted_iota(I32, (HEAD, SIDE), 1)
    heads = [r[SLOTS * SIDE :, :].astype(F32) for r in ins]
    for db in range(RING):
        head = jnp.zeros((HEAD, SIDE), F32)
        for da in range(RING):
            outs[db][da * CAP * SIDE : (da + 1) * CAP * SIDE, :] = ins[da][db * CAP * SIDE : (db + 1) * CAP * SIDE, :]
            turned = pltpu.roll(heads[da], ((da - db) * CAP) % SIDE, 1)
            head = jnp.where((lanes >= da * CAP) & (lanes < (da + 1) * CAP), turned, head)
        outs[db][SLOTS * SIDE :, :] = head.astype(BF16)


def turn(parts, after):
    return pl.pallas_call(
        turn_kernel,
        in_specs=[ANY] + [VMEM] * RING,
        out_specs=[VMEM] * RING,
        out_shape=[pltpu.VMEM((MSG, SIDE), BF16)] * RING,
        compiler_params=params(8),
        name="turn",
    )(after, *[kept(v) for v in parts])


def order(da, db):
    travels = jnp.where(da == 2, 0, jnp.where(da == 1, 3, 6)) + db - 1
    return jnp.where(da == 0, 12 + db, jnp.where(db == 0, 8 + da, travels))


def group(pieces, info_v, info_s, packed):
    first, a, b = place()
    n = len(pieces) * RING * SLOTS
    lanes = lax.broadcasted_iota(I32, (8, SIDE), 1)
    head = jnp.zeros((8, SIDE), F32)
    for i in range(len(pieces) * RING):
        at = (i % RING) * MSG + SLOTS * SIDE
        one = pieces[i // RING][at : at + HEAD, :].astype(F32)[0:8]
        here = (lanes >= i * SLOTS) & (lanes < (i + 1) * SLOTS)
        head = jnp.where(here, pltpu.roll(one, i * SLOTS, 1) if i else one, head)
    occ = jnp.broadcast_to(head[0:1], (8, SIDE)).astype(I32) - 1
    loc = jnp.broadcast_to(head[1:2], (8, SIDE)).astype(I32)
    da, db = relative(occ, first, a, b)
    block = jnp.where(occ >= 0, order(da, db), DUMMY)
    rows = lax.broadcasted_iota(I32, (SIDE, SIDE), 0)
    cols = lax.broadcasted_iota(I32, (SIDE, SIDE), 1)
    hot = (rows == jnp.broadcast_to(block[0:1], (SIDE, SIDE))) & (rows < OCC)
    hot = jnp.where(hot, 1.0, 0.0)
    count = jnp.broadcast_to(jnp.sum(hot, axis=1, keepdims=True), (SIDE, SIDE)).astype(I32)
    padded = (((count + 1) >> 1) << 1).astype(F32)
    below = jnp.where(cols < rows, 1.0, 0.0).astype(BF16)
    above = jnp.where(rows < cols, 1.0, 0.0).astype(BF16)
    start = jnp.dot(below, padded.astype(BF16), preferred_element_type=F32)
    rank = jnp.dot(hot.astype(BF16), above, preferred_element_type=F32)
    spot = jnp.broadcast_to(jnp.sum(hot * (start + rank), axis=0, keepdims=True), (8, SIDE)).astype(I32)
    spot = jnp.where(occ >= 0, spot, n + OCC)
    rows8 = lax.broadcasted_iota(I32, (8, SIDE), 0)
    info_v[0:8, :] = jnp.where(rows8 == 0, spot, jnp.where(rows8 == 1, loc, block))
    start = start.astype(I32)
    info_v[8:INFO, :] = jnp.where(cols == 0, start, start + count)[0 : INFO - 8, :]
    pltpu.sync_copy(info_v, info_s)
    for i in range(OCC):
        free = pl.multiple_of(info_s[8 + i, 1] * SIDE, SIDE)
        packed[pl.ds(free, SIDE), :] = jnp.zeros((SIDE, SIDE), BF16)
    for i in range(n):
        to = pl.multiple_of(info_s[0, i] * SIDE, SIDE)
        at = (i // SLOTS % RING) * MSG + (i % SLOTS) * SIDE
        packed[pl.ds(to, SIDE), :] = pieces[i // (RING * SLOTS)][at : at + SIDE, :]


def read_lists(n, info_s, loc_s, block_s):
    for i in range(OCC):
        loc_s[info_s[8 + i, 1]] = 0
    for i in range(n):
        to = info_s[0, i]
        loc_s[to] = info_s[1, i]
        block_s[to] = info_s[2, i]


def multiply(blocks, info_s, loc_s, block_s, packed, ints, total):
    begin = info_s[8 + blocks[0], 0] >> 1
    end = info_s[8 + blocks[1], 0] >> 1

    def body(i, carry):
        for u in range(UNROLL):
            pair = begin + i * UNROLL + u
            k = jnp.minimum(pair, end - 1) * 2
            block = jnp.where(pair < end, block_s[k], DUMMY)
            at = pl.multiple_of(block * SIDE, SIDE)
            tiles = [packed[pl.ds(pl.multiple_of((k + j) * SIDE, SIDE), SIDE), :] for j in range(2)]
            rows = [ints[pl.ds(pl.multiple_of(loc_s[k + j] * SIDE, SIDE), SIDE), :] for j in range(2)]
            total[pl.ds(at, SIDE), :] += jnp.dot(
                jnp.concatenate(tiles, axis=1), jnp.concatenate(rows, axis=0), preferred_element_type=F32
            )
        return carry

    lax.fori_loop(0, (end - begin + UNROLL - 1) // UNROLL, body, 0)


def spots(n):
    return n * RING * SLOTS + OCC + 2


def list_scratch(n):
    return [pltpu.SMEM((INFO, SIDE), I32), pltpu.SMEM((spots(n),), I32), pltpu.SMEM((spots(n),), I32)]


def cost(flops):
    return pl.CostEstimate(flops=flops, bytes_accessed=2**12, transcendentals=0)


def accumulate(total, ints, pieces):
    n = len(pieces)
    old = [] if total is None else [total]

    def kernel(*refs):
        refs = refs[len(old) :]
        ints_ref, piece_refs, acc = refs[0], refs[1 : 1 + n], refs[1 + n]
        packed, info_v, info_s, loc_s, block_s = refs[2 + n :]
        if not old:
            acc[...] = jnp.zeros_like(acc)
        group(piece_refs, info_v, info_s, packed)
        read_lists(n * RING * SLOTS, info_s, loc_s, block_s)
        multiply((0, OCC), info_s, loc_s, block_s, packed, ints_ref, acc)

    return pl.pallas_call(
        kernel,
        in_specs=[VMEM] * (len(old) + 1 + n),
        out_specs=VMEM,
        out_shape=pltpu.VMEM(((OCC + 1) * SIDE, ints.shape[1]), F32),
        scratch_shapes=[pltpu.VMEM((spots(n) * SIDE, SIDE), BF16), pltpu.VMEM((INFO, SIDE), I32)] + list_scratch(n),
        input_output_aliases={0: 0} if old else {},
        compiler_params=params(14),
        cost_estimate=cost(2**20),
        name="accumulate",
    )(*[kept(v) for v in old], kept(ints), *[kept(v) for v in pieces])


def finish(total, ints, late, blocks, outs, flops):
    n = RING
    width = ints.shape[1]
    new = len(late) == n
    given = [pltpu.VMEM((spots(n) * SIDE, SIDE), BF16), pltpu.VMEM((INFO, SIDE), I32)] if new else []

    def kernel(total_in, ints_ref, *refs):
        late_refs, acc, out_refs, rest = refs[: len(late)], refs[len(late)], refs[len(late) + 1 :][: len(outs)], refs[len(late) + 1 + len(outs) :]
        if new:
            packed, info_v, info_s, loc_s, block_s = rest
            group(late_refs, info_v, info_s, packed)
        else:
            packed, info_v = late_refs
            info_s, loc_s, block_s = rest
            pltpu.sync_copy(info_v, info_s)
        read_lists(n * RING * SLOTS, info_s, loc_s, block_s)
        multiply(blocks, info_s, loc_s, block_s, packed, ints_ref, acc)
        for ref, (start, many) in zip(out_refs, outs):
            ref[...] = acc[start * SIDE : (start + many) * SIDE, :].astype(BF16)

    total, *results = pl.pallas_call(
        kernel,
        in_specs=[VMEM] * (2 + len(late)),
        out_specs=[VMEM] * (1 + len(outs) + len(given)),
        out_shape=[pltpu.VMEM(total.shape, F32)] + [pltpu.VMEM((many * SIDE, width), BF16) for _, many in outs] + given,
        scratch_shapes=list_scratch(n),
        input_output_aliases={0: 0},
        compiler_params=params(8),
        cost_estimate=cost(flops),
        name="finish",
    )(kept(total), kept(ints), *[kept(v) for v in late])
    return total, results[: len(outs)], results[len(outs) :] if new else late


def fold(total, start, many, others, cut, dtype, space):
    width = total.shape[1]
    rows = many * SIDE // cut

    def kernel(total_ref, *refs):
        ins, outs = refs[: len(others)], refs[len(others) :]
        for c, out in enumerate(outs):
            value = total_ref[start * SIDE + c * rows : start * SIDE + (c + 1) * rows, :]
            for ref in ins:
                value = value + ref[c * rows : (c + 1) * rows, :].astype(F32)
            out[...] = value.astype(dtype)

    return pl.pallas_call(
        kernel,
        in_specs=[VMEM] * (1 + len(others)),
        out_specs=[VMEM] * cut,
        out_shape=[space((rows, width), dtype)] * cut,
        compiler_params=params(8),
        cost_estimate=cost(2**20),
        name="fold",
    )(kept(total), *[kept(v) for v in others])


def first_steps(parts):
    return [parts[0]] + [send_first(parts[d], d) for d in (1, 2, 3)]


def second_steps(parts):
    return jnp.concatenate([parts[0]] + [send_second(parts[d], d) for d in (1, 2, 3)], axis=0)


def per_device(amp_tiles, owner_col, local_pair, occ_pair, integrals):
    *parts, raw = sort_own(owner_col[:, 0], local_pair, occ_pair, amp_tiles)
    far_raw = send_y(raw, 2)
    parts = first_steps(parts)
    turned = turn(parts, parts[0])
    own = second_steps(turned)
    up, down, own_other = send_y(own, 1), send_y(own, -1), send_core(own)
    far_parts = sort_far(far_raw, turned[0])
    far = second_steps(turn(first_steps(far_parts), own))
    total = accumulate(None, integrals, [own, own_other])
    up, down, total = lax.optimization_barrier((up, down, total))
    late = [up, down, send_core(up), send_core(down)]
    total = accumulate(total, integrals, [far, send_core(far)])

    total, (to_2,), late = finish(total, integrals, late, (0, 3), [(0, 3)], 2**31)
    got = [send_first(to_2, 2)]
    total, (to_1, to_3), late = finish(total, integrals, late, (3, 9), [(3, 3), (6, 3)], 2**31)
    got += [send_first(to_1, 1), send_first(to_3, -1)]
    total, lasts, late = finish(total, integrals, late, (9, 12), [(9, 1), (10, 1), (11, 1)], 2**31)
    got_last = [send_first(lasts[1], 2), send_first(lasts[0], 1), send_first(lasts[2], -1)]
    total, _, late = finish(total, integrals, late, (12, 16), [], 2**31)
    rest = fold(total, 13, 3, got, 3, BF16, pltpu.VMEM)
    got_last += [send_second(rest[d - 1], d) for d in (2, 1, 3)]
    return fold(total, 12, 1, got_last, 1, BF16, jax.ShapeDtypeStruct)[0]


def solution(mesh):
    return jax.shard_map(
        per_device,
        mesh=mesh,
        in_specs=(
            P(("row", "col"), None, None),
            P(("row", "col"), None),
            P(("row", "col")),
            P(("row", "col")),
            P("col", "row"),
        ),
        out_specs=P("col", "row"),
        check_vma=False,
    )
```

```python
import jax
import jax.numpy as jnp
from jax import lax
from jax.experimental import pallas as pl
from jax.experimental.pallas import tpu as pltpu
from jax.sharding import PartitionSpec as P

SIDE = 128
CAP = 2
RING = 4
SLOTS = RING * CAP
HEAD = 16
MSG = SLOTS * SIDE + HEAD
PIECE = RING * MSG
OCC = RING * RING
DUMMY = OCC
UNROLL = 4
INFO = 32

VMEM = pl.BlockSpec(memory_space=pltpu.VMEM)
SMEM = pl.BlockSpec(memory_space=pltpu.SMEM)
ANY = pl.BlockSpec(memory_space=pl.ANY)
HBM = pl.BlockSpec(memory_space=pltpu.HBM)
F32, BF16, I32 = jnp.float32, jnp.bfloat16, jnp.int32


def row_perm(step):
    return [(r, (r + 2 * step) % (2 * RING)) for r in range(2 * RING)]


CORE_PERM = [(r, r ^ 1) for r in range(2 * RING)]


def plane_perm(step, second):
    pairs = []
    for r in range(2 * RING):
        for x in range(RING):
            for z in range(RING):
                along_x = (r % 2 == 0) != second
                nx, nz = ((x + step) % RING, z) if along_x else (x, (z + step) % RING)
                pairs.append((r * OCC + x * RING + z, r * OCC + nx * RING + nz))
    return pairs


def send_first(v, step):
    return lax.ppermute(v, ("row", "col"), plane_perm(step, False))


def send_second(v, step):
    return lax.ppermute(v, ("row", "col"), plane_perm(step, True))


def send_y(v, step):
    return lax.ppermute(v, "row", row_perm(step))


def send_core(v):
    return lax.ppermute(v, "row", CORE_PERM)


def place():
    core = lax.rem(lax.axis_index("row"), 2)
    col = lax.axis_index("col")
    x, z = col // RING, lax.rem(col, RING)
    first = core == 0
    return first, jnp.where(first, x, z), jnp.where(first, z, x)


def relative(index, first, a, b):
    x, z = index >> 2, index & 3
    return (jnp.where(first, x, z) - a) & 3, (jnp.where(first, z, x) - b) & 3


def params(mib):
    return pltpu.CompilerParams(vmem_limit_bytes=mib * 2**20)


def kept(v):
    return pltpu.with_memory_space_constraint(v, pltpu.VMEM)


def in_hbm(v):
    return pltpu.with_memory_space_constraint(v, pltpu.HBM)


def header(lines):
    rows = lax.broadcasted_iota(I32, (HEAD, SIDE), 0)
    head = jnp.zeros((HEAD, SIDE), F32)
    for i, line in enumerate(lines):
        head = jnp.where(rows == i, jnp.broadcast_to(line, (HEAD, SIDE)), head)
    return head.astype(BF16)


def sort_tiles_body(owner_of, loc_at, occ_at, tile_at, count, outs, seen):
    first, a, b = place()
    for o in range(OCC):
        seen[o] = 0
    rows = lax.broadcasted_iota(I32, (8, SIDE), 0)
    lanes = lax.broadcasted_iota(I32, (8, SIDE), 1)
    occ_of = jnp.zeros((8, SIDE), F32)
    loc_of = jnp.zeros((8, SIDE), F32)
    for k in range(count):
        owner = owner_of(k)
        rank = seen[owner]
        seen[owner] = rank + 1
        da, db = relative(owner, first, a, b)
        slot = db * CAP + rank
        here = (rows == da) & (lanes == slot)
        occ_of = jnp.where(here, (occ_at(k) + 1).astype(F32), occ_of)
        loc_of = jnp.where(here, loc_at(k).astype(F32), loc_of)
        at = pl.ds(pl.multiple_of(slot * SIDE, SIDE), SIDE)
        for d in range(RING):

            @pl.when(da == d)
            def _(d=d, k=k, at=at):
                outs[d][at, :] = tile_at(k)

    for d in range(RING):
        outs[d][SLOTS * SIDE :, :] = header([occ_of[d : d + 1], loc_of[d : d + 1]])


def sort_own(owner, loc, occ, tiles):
    count = tiles.shape[0]

    def kernel(owner_hbm, loc_hbm, occ_hbm, tiles_hbm, *refs):
        outs, raw, seen = refs[:RING], refs[RING], refs[RING + 1]
        owner_ref, loc_ref, occ_ref, sems = refs[RING + 2 :]
        pairs = [(owner_hbm, owner_ref), (loc_hbm, loc_ref), (occ_hbm, occ_ref)]
        pairs += [(tiles_hbm.at[k], raw.at[pl.ds(k * SIDE, SIDE), :]) for k in range(count)]
        copies = [pltpu.make_async_copy(src, dst, sems.at[i]) for i, (src, dst) in enumerate(pairs)]
        for copy in copies:
            copy.start()
        for copy in copies:
            copy.wait()
        sort_tiles_body(
            lambda k: owner_ref[k],
            lambda k: loc_ref[k],
            lambda k: occ_ref[k],
            lambda k: raw[k * SIDE : (k + 1) * SIDE, :],
            count,
            outs,
            seen,
        )
        lanes = lax.broadcasted_iota(I32, (8, SIDE), 1)
        rows = []
        for ref in (owner_ref, loc_ref, occ_ref):
            row = jnp.zeros((8, SIDE), F32)
            for k in range(count):
                row = jnp.where(lanes == k, ref[k].astype(F32), row)
            rows.append(row[0:1])
        raw[count * SIDE :, :] = header(rows)

    return pl.pallas_call(
        kernel,
        in_specs=[HBM] * 4,
        out_specs=[VMEM] * (RING + 1),
        out_shape=[pltpu.VMEM((MSG, SIDE), BF16)] * RING + [pltpu.VMEM((count * SIDE + HEAD, SIDE), BF16)],
        scratch_shapes=[pltpu.SMEM((OCC,), I32)]
        + [pltpu.SMEM((count,), I32)] * 3
        + [pltpu.SemaphoreType.DMA((3 + count,))],
        compiler_params=params(8),
        name="sort_own",
    )(*[in_hbm(v) for v in (owner, loc, occ, tiles)])


def sort_far(raw, after):
    count = (raw.shape[0] - HEAD) // SIDE

    def kernel(raw_ref, after_ref, *refs):
        outs, seen, head_v, head_s = refs[:RING], refs[RING], refs[RING + 1], refs[RING + 2]
        head_v[...] = raw_ref[count * SIDE :, :].astype(F32)[0:8].astype(I32)
        pltpu.sync_copy(head_v, head_s)
        sort_tiles_body(
            lambda k: head_s[0, k],
            lambda k: head_s[1, k],
            lambda k: head_s[2, k],
            lambda k: raw_ref[k * SIDE : (k + 1) * SIDE, :],
            count,
            outs,
            seen,
        )

    return pl.pallas_call(
        kernel,
        in_specs=[VMEM, ANY],
        out_specs=[VMEM] * RING,
        out_shape=[pltpu.VMEM((MSG, SIDE), BF16)] * RING,
        scratch_shapes=[pltpu.SMEM((OCC,), I32), pltpu.VMEM((8, SIDE), I32), pltpu.SMEM((8, SIDE), I32)],
        compiler_params=params(8),
        name="sort_far",
    )(kept(raw), after)


def turn_kernel(after, *refs):
    ins, outs = refs[:RING], refs[RING:]
    lanes = lax.broadcasted_iota(I32, (HEAD, SIDE), 1)
    heads = [r[SLOTS * SIDE :, :].astype(F32) for r in ins]
    for db in range(RING):
        head = jnp.zeros((HEAD, SIDE), F32)
        for da in range(RING):
            outs[db][da * CAP * SIDE : (da + 1) * CAP * SIDE, :] = ins[da][db * CAP * SIDE : (db + 1) * CAP * SIDE, :]
            turned = pltpu.roll(heads[da], ((da - db) * CAP) % SIDE, 1)
            head = jnp.where((lanes >= da * CAP) & (lanes < (da + 1) * CAP), turned, head)
        outs[db][SLOTS * SIDE :, :] = head.astype(BF16)


def turn(parts, after):
    return pl.pallas_call(
        turn_kernel,
        in_specs=[ANY] + [VMEM] * RING,
        out_specs=[VMEM] * RING,
        out_shape=[pltpu.VMEM((MSG, SIDE), BF16)] * RING,
        compiler_params=params(8),
        name="turn",
    )(after, *[kept(v) for v in parts])


def order(da, db):
    ahead = jnp.where(db >= 2, 2 + db, 8 + db)
    behind = jnp.where(db >= 2, 8 + db, 6 + db)
    return jnp.where(da == 0, 12 + db, jnp.where(da == 2, db, jnp.where(da == 1, ahead, behind)))


def message_places(pieces):
    return [(piece, m * MSG) for piece in pieces for m in range(piece.shape[0] // MSG)]


def group(pieces, info_v, info_s, packed):
    first, a, b = place()
    messages = message_places(pieces)
    n = len(messages) * SLOTS
    lanes = lax.broadcasted_iota(I32, (8, SIDE), 1)
    head = jnp.zeros((8, SIDE), F32)
    for i, (piece, at) in enumerate(messages):
        at += SLOTS * SIDE
        one = piece[at : at + HEAD, :].astype(F32)[0:8]
        here = (lanes >= i * SLOTS) & (lanes < (i + 1) * SLOTS)
        head = jnp.where(here, pltpu.roll(one, i * SLOTS, 1) if i else one, head)
    occ = jnp.broadcast_to(head[0:1], (8, SIDE)).astype(I32) - 1
    loc = jnp.broadcast_to(head[1:2], (8, SIDE)).astype(I32)
    da, db = relative(occ, first, a, b)
    block = jnp.where(occ >= 0, order(da, db), DUMMY)
    rows = lax.broadcasted_iota(I32, (SIDE, SIDE), 0)
    cols = lax.broadcasted_iota(I32, (SIDE, SIDE), 1)
    hot = (rows == jnp.broadcast_to(block[0:1], (SIDE, SIDE))) & (rows < OCC)
    hot = jnp.where(hot, 1.0, 0.0)
    count = jnp.broadcast_to(jnp.sum(hot, axis=1, keepdims=True), (SIDE, SIDE)).astype(I32)
    padded = (((count + 1) >> 1) << 1).astype(F32)
    below = jnp.where(cols < rows, 1.0, 0.0).astype(BF16)
    above = jnp.where(rows < cols, 1.0, 0.0).astype(BF16)
    start = jnp.dot(below, padded.astype(BF16), preferred_element_type=F32)
    rank = jnp.dot(hot.astype(BF16), above, preferred_element_type=F32)
    spot = jnp.broadcast_to(jnp.sum(hot * (start + rank), axis=0, keepdims=True), (8, SIDE)).astype(I32)
    spot = jnp.where(occ >= 0, spot, n + OCC)
    rows8 = lax.broadcasted_iota(I32, (8, SIDE), 0)
    info_v[0:8, :] = jnp.where(rows8 == 0, spot, jnp.where(rows8 == 1, loc, block))
    start = start.astype(I32)
    info_v[8:INFO, :] = jnp.where(cols == 0, start, start + count)[0 : INFO - 8, :]
    pltpu.sync_copy(info_v, info_s)
    for i in range(OCC):
        free = pl.multiple_of(info_s[8 + i, 1] * SIDE, SIDE)
        packed[pl.ds(free, SIDE), :] = jnp.zeros((SIDE, SIDE), BF16)
    for i in range(n):
        to = pl.multiple_of(info_s[0, i] * SIDE, SIDE)
        piece, at = messages[i // SLOTS]
        at += i % SLOTS * SIDE
        packed[pl.ds(to, SIDE), :] = piece[at : at + SIDE, :]


def read_lists(n, info_s, loc_s, block_s):
    for i in range(OCC):
        loc_s[info_s[8 + i, 1]] = 0
    for i in range(n):
        to = info_s[0, i]
        loc_s[to] = info_s[1, i]
        block_s[to] = info_s[2, i]


def multiply(blocks, info_s, loc_s, block_s, packed, ints, total):
    begin = info_s[8 + blocks[0], 0] >> 1
    end = info_s[8 + blocks[1], 0] >> 1

    def body(i, carry):
        for u in range(UNROLL):
            pair = begin + i * UNROLL + u
            k = jnp.minimum(pair, end - 1) * 2
            block = jnp.where(pair < end, block_s[k], DUMMY)
            at = pl.multiple_of(block * SIDE, SIDE)
            tiles = [packed[pl.ds(pl.multiple_of((k + j) * SIDE, SIDE), SIDE), :] for j in range(2)]
            rows = [ints[pl.ds(pl.multiple_of(loc_s[k + j] * SIDE, SIDE), SIDE), :] for j in range(2)]
            total[pl.ds(at, SIDE), :] += jnp.dot(
                jnp.concatenate(tiles, axis=1), jnp.concatenate(rows, axis=0), preferred_element_type=F32
            )
        return carry

    lax.fori_loop(0, (end - begin + UNROLL - 1) // UNROLL, body, 0)


def spots(n):
    return n + OCC + 2


def list_scratch(n):
    return [pltpu.SMEM((INFO, SIDE), I32), pltpu.SMEM((spots(n),), I32), pltpu.SMEM((spots(n),), I32)]


def cost(flops):
    return pl.CostEstimate(flops=flops, bytes_accessed=2**12, transcendentals=0)


def accumulate(total, ints, pieces):
    many = len(pieces)
    n = len(message_places(pieces)) * SLOTS
    old = [] if total is None else [total]

    def kernel(*refs):
        refs = refs[len(old) :]
        ints_ref, piece_refs, acc = refs[0], refs[1 : 1 + many], refs[1 + many]
        packed, info_v, info_s, loc_s, block_s = refs[2 + many :]
        if not old:
            acc[...] = jnp.zeros_like(acc)
        group(piece_refs, info_v, info_s, packed)
        read_lists(n, info_s, loc_s, block_s)
        multiply((0, OCC), info_s, loc_s, block_s, packed, ints_ref, acc)

    return pl.pallas_call(
        kernel,
        in_specs=[VMEM] * (len(old) + 1 + many),
        out_specs=VMEM,
        out_shape=pltpu.VMEM(((OCC + 1) * SIDE, ints.shape[1]), F32),
        scratch_shapes=[pltpu.VMEM((spots(n) * SIDE, SIDE), BF16), pltpu.VMEM((INFO, SIDE), I32)] + list_scratch(n),
        input_output_aliases={0: 0} if old else {},
        compiler_params=params(14),
        cost_estimate=cost(2**20),
        name="accumulate",
    )(*[kept(v) for v in old], kept(ints), *[kept(v) for v in pieces])


def finish(total, ints, late, blocks, outs, flops):
    new = late[1].dtype == BF16
    n = len(message_places(late)) * SLOTS if new else late[0].shape[0] // SIDE - OCC - 2
    width = ints.shape[1]
    given = [pltpu.VMEM((spots(n) * SIDE, SIDE), BF16), pltpu.VMEM((INFO, SIDE), I32)] if new else []

    def kernel(total_in, ints_ref, *refs):
        late_refs, acc, out_refs, rest = refs[: len(late)], refs[len(late)], refs[len(late) + 1 :][: len(outs)], refs[len(late) + 1 + len(outs) :]
        if new:
            packed, info_v, info_s, loc_s, block_s = rest
            group(late_refs, info_v, info_s, packed)
        else:
            packed, info_v = late_refs
            info_s, loc_s, block_s = rest
            pltpu.sync_copy(info_v, info_s)
        read_lists(n, info_s, loc_s, block_s)
        multiply(blocks, info_s, loc_s, block_s, packed, ints_ref, acc)
        for ref, (start, many) in zip(out_refs, outs):
            ref[...] = acc[start * SIDE : (start + many) * SIDE, :].astype(BF16)

    total, *results = pl.pallas_call(
        kernel,
        in_specs=[VMEM] * (2 + len(late)),
        out_specs=[VMEM] * (1 + len(outs) + len(given)),
        out_shape=[pltpu.VMEM(total.shape, F32)] + [pltpu.VMEM((many * SIDE, width), BF16) for _, many in outs] + given,
        scratch_shapes=list_scratch(n),
        input_output_aliases={0: 0},
        compiler_params=params(8),
        cost_estimate=cost(flops),
        name="finish",
    )(kept(total), kept(ints), *[kept(v) for v in late])
    return total, results[: len(outs)], results[len(outs) :] if new else late


def fold(total, others, outs, dtype, space):
    width = total.shape[1]

    def kernel(total_ref, *refs):
        for (start, many, terms), out in zip(outs, refs[len(others) :]):
            value = total_ref[start * SIDE : (start + many) * SIDE, :]
            for which, at in terms:
                value = value + refs[which][at * SIDE : (at + many) * SIDE, :].astype(F32)
            out[...] = value.astype(dtype)

    return pl.pallas_call(
        kernel,
        in_specs=[VMEM] * (1 + len(others)),
        out_specs=[VMEM] * len(outs),
        out_shape=[space((many * SIDE, width), dtype) for _, many, _ in outs],
        compiler_params=params(8),
        cost_estimate=cost(2**20),
        name="fold",
    )(kept(total), *[kept(v) for v in others])


def first_steps(parts):
    return [parts[0]] + [send_first(parts[d], d) for d in (1, 2, 3)]


def second_steps(parts):
    return [parts[0]] + [send_second(parts[d], d) for d in (1, 2, 3)]


def join(parts, after):
    sizes = [v.shape[0] for v in parts]

    def kernel(after_ref, *refs):
        at = 0
        for ref, size in zip(refs, sizes):
            refs[-1][at : at + size, :] = ref[...]
            at += size

    return pl.pallas_call(
        kernel,
        in_specs=[ANY] + [VMEM] * len(parts),
        out_specs=VMEM,
        out_shape=pltpu.VMEM((sum(sizes), SIDE), BF16),
        compiler_params=params(8),
        cost_estimate=cost(2**20),
        name="join",
    )(after, *[kept(v) for v in parts])


def hold(parts, after):
    def kernel(after_ref, *refs):
        for src, dst in zip(refs, refs[len(parts) :]):
            dst[...] = src[...]

    return pl.pallas_call(
        kernel,
        in_specs=[ANY] + [VMEM] * len(parts),
        out_specs=[VMEM] * len(parts),
        out_shape=[pltpu.VMEM(v.shape, BF16) for v in parts],
        compiler_params=params(8),
        cost_estimate=cost(2**20),
        name="hold",
    )(after, *[kept(v) for v in parts])


def load(ints):
    def kernel(src, dst, sem):
        copy = pltpu.make_async_copy(src, dst, sem)
        copy.start()
        copy.wait()

    return pl.pallas_call(
        kernel,
        in_specs=[HBM],
        out_specs=VMEM,
        out_shape=pltpu.VMEM(ints.shape, ints.dtype),
        scratch_shapes=[pltpu.SemaphoreType.DMA],
        compiler_params=params(8),
        cost_estimate=cost(2**20),
        name="load",
    )(in_hbm(ints))


def per_device(amp_tiles, owner_col, local_pair, occ_pair, integrals):
    *parts, raw = sort_own(owner_col[:, 0], local_pair, occ_pair, amp_tiles)
    far_raw = send_y(raw, 2)
    ints = load(integrals)
    turned = turn(first_steps(parts), ints)
    near = second_steps(turned)
    own = jnp.concatenate(near, axis=0)
    up, down = send_y(own, 1), send_y(own, -1)
    far_parts = sort_far(far_raw, turned[0])
    far_turned = turn(first_steps(far_parts), own)
    far = second_steps(far_turned)
    total = accumulate(None, ints, [own] + [send_core(v) for v in near])
    far_other = [send_core(v) for v in [join(far[:1], total)] + far[1:]]
    total = accumulate(total, ints, far + far_other)
    up, down, total = lax.optimization_barrier((up, down, total))
    late = [send_core(up), send_core(down)]
    total = accumulate(total, ints, [up, down])

    total, (two_ahead, two_behind), late = finish(total, ints, late, (0, 4), [(0, 2), (2, 2)], 2**31)
    from_behind, from_ahead = send_first(two_ahead, 1), send_first(two_behind, -1)
    total, (ahead, behind), late = finish(total, ints, late, (4, 8), [(4, 2), (6, 2)], 2**31)
    got = [send_first(behind, -1), send_first(ahead, 1)]
    total, _, late = finish(total, ints, late, (8, 12), [], 2**31)
    ahead, behind = fold(total, [from_behind, from_ahead], [(8, 2, [(0, 0)]), (10, 2, [(1, 0)])], BF16, pltpu.VMEM)
    got += [send_first(ahead, 1), send_first(behind, -1)]
    total, _, late = finish(total, ints, late, (12, 16), [], 2**31)
    outs = [(13, 1, [(0, 1), (2, 1)]), (14, 1, [(1, 0), (3, 0)]), (15, 1, [(1, 1), (3, 1)])]
    rest = fold(total, got, outs, BF16, pltpu.VMEM)
    last = [got[0], got[2]] + [send_second(rest[d - 1], d) for d in (2, 1, 3)]
    return fold(total, last, [(12, 1, [(i, 0) for i in range(5)])], BF16, jax.ShapeDtypeStruct)[0]


def solution(mesh):
    return jax.shard_map(
        per_device,
        mesh=mesh,
        in_specs=(
            P(("row", "col"), None, None),
            P(("row", "col"), None),
            P(("row", "col")),
            P(("row", "col")),
            P("col", "row"),
        ),
        out_specs=P("col", "row"),
        check_vma=False,
    )
```

```python
import jax
import jax.numpy as jnp
from jax import lax
from jax.experimental import pallas as pl
from jax.experimental.pallas import tpu as pltpu
from jax.sharding import PartitionSpec as P

SIDE = 128
CAP = 2
RING = 4
SLOTS = RING * CAP
HEAD = 16
MSG = SLOTS * SIDE + HEAD
PIECE = RING * MSG
OCC = RING * RING
STEPS = (0, 2, 1, 3)
DUMMY = OCC
UNROLL = 4
INFO = 32

VMEM = pl.BlockSpec(memory_space=pltpu.VMEM)
SMEM = pl.BlockSpec(memory_space=pltpu.SMEM)
ANY = pl.BlockSpec(memory_space=pl.ANY)
HBM = pl.BlockSpec(memory_space=pltpu.HBM)
F32, BF16, I32 = jnp.float32, jnp.bfloat16, jnp.int32


def row_perm(step):
    return [(r, (r + 2 * step) % (2 * RING)) for r in range(2 * RING)]


CORE_PERM = [(r, r ^ 1) for r in range(2 * RING)]


def plane_perm(step, second):
    pairs = []
    for r in range(2 * RING):
        for x in range(RING):
            for z in range(RING):
                along_x = (r % 2 == 0) != second
                nx, nz = ((x + step) % RING, z) if along_x else (x, (z + step) % RING)
                pairs.append((r * OCC + x * RING + z, r * OCC + nx * RING + nz))
    return pairs


def send_first(v, step):
    return lax.ppermute(v, ("row", "col"), plane_perm(step, False))


def send_second(v, step):
    return lax.ppermute(v, ("row", "col"), plane_perm(step, True))


def send_y(v, step):
    return lax.ppermute(v, "row", row_perm(step))


def send_core(v):
    return lax.ppermute(v, "row", CORE_PERM)


def place():
    core = lax.rem(lax.axis_index("row"), 2)
    col = lax.axis_index("col")
    x, z = col // RING, lax.rem(col, RING)
    first = core == 0
    return first, jnp.where(first, x, z), jnp.where(first, z, x)


def relative(index, first, a, b):
    x, z = index >> 2, index & 3
    return (jnp.where(first, x, z) - a) & 3, (jnp.where(first, z, x) - b) & 3


def params(mib):
    return pltpu.CompilerParams(vmem_limit_bytes=mib * 2**20)


def kept(v):
    return pltpu.with_memory_space_constraint(v, pltpu.VMEM)


def in_hbm(v):
    return pltpu.with_memory_space_constraint(v, pltpu.HBM)


def header(lines):
    rows = lax.broadcasted_iota(I32, (HEAD, SIDE), 0)
    head = jnp.zeros((HEAD, SIDE), F32)
    for i, line in enumerate(lines):
        head = jnp.where(rows == i, jnp.broadcast_to(line, (HEAD, SIDE)), head)
    return head.astype(BF16)


def sort_tiles_body(owner_of, loc_at, occ_at, tile_at, count, outs, seen):
    first, a, b = place()
    for o in range(OCC):
        seen[o] = 0
    rows = lax.broadcasted_iota(I32, (8, SIDE), 0)
    lanes = lax.broadcasted_iota(I32, (8, SIDE), 1)
    occ_of = jnp.zeros((8, SIDE), F32)
    loc_of = jnp.zeros((8, SIDE), F32)
    for k in range(count):
        owner = owner_of(k)
        rank = seen[owner]
        seen[owner] = rank + 1
        da, db = relative(owner, first, a, b)
        slot = db * CAP + rank
        here = (rows == da) & (lanes == slot)
        occ_of = jnp.where(here, (occ_at(k) + 1).astype(F32), occ_of)
        loc_of = jnp.where(here, loc_at(k).astype(F32), loc_of)
        at = pl.ds(pl.multiple_of(slot * SIDE, SIDE), SIDE)
        for d in range(RING):

            @pl.when(da == d)
            def _(d=d, k=k, at=at):
                outs[d][at, :] = tile_at(k)

    for d in range(RING):
        outs[d][SLOTS * SIDE :, :] = header([occ_of[d : d + 1], loc_of[d : d + 1]])


def sort_own(owner, loc, occ, tiles):
    count = tiles.shape[0]

    def kernel(owner_hbm, loc_hbm, occ_hbm, tiles_hbm, *refs):
        outs, raw, seen = refs[:RING], refs[RING], refs[RING + 1]
        owner_ref, loc_ref, occ_ref, sems = refs[RING + 2 :]
        pairs = [(owner_hbm, owner_ref), (loc_hbm, loc_ref), (occ_hbm, occ_ref)]
        pairs += [(tiles_hbm.at[k], raw.at[pl.ds(k * SIDE, SIDE), :]) for k in range(count)]
        copies = [pltpu.make_async_copy(src, dst, sems.at[i]) for i, (src, dst) in enumerate(pairs)]
        for copy in copies:
            copy.start()
        for copy in copies:
            copy.wait()
        sort_tiles_body(
            lambda k: owner_ref[k],
            lambda k: loc_ref[k],
            lambda k: occ_ref[k],
            lambda k: raw[k * SIDE : (k + 1) * SIDE, :],
            count,
            outs,
            seen,
        )
        lanes = lax.broadcasted_iota(I32, (8, SIDE), 1)
        rows = []
        for ref in (owner_ref, loc_ref, occ_ref):
            row = jnp.zeros((8, SIDE), F32)
            for k in range(count):
                row = jnp.where(lanes == k, ref[k].astype(F32), row)
            rows.append(row[0:1])
        raw[count * SIDE :, :] = header(rows)

    return pl.pallas_call(
        kernel,
        in_specs=[HBM] * 4,
        out_specs=[VMEM] * (RING + 1),
        out_shape=[pltpu.VMEM((MSG, SIDE), BF16)] * RING + [pltpu.VMEM((count * SIDE + HEAD, SIDE), BF16)],
        scratch_shapes=[pltpu.SMEM((OCC,), I32)]
        + [pltpu.SMEM((count,), I32)] * 3
        + [pltpu.SemaphoreType.DMA((3 + count,))],
        compiler_params=params(8),
        name="sort_own",
    )(*[in_hbm(v) for v in (owner, loc, occ, tiles)])


def sort_far(raw, after):
    count = (raw.shape[0] - HEAD) // SIDE

    def kernel(raw_ref, after_ref, *refs):
        outs, seen, head_v, head_s = refs[:RING], refs[RING], refs[RING + 1], refs[RING + 2]
        head_v[...] = raw_ref[count * SIDE :, :].astype(F32)[0:8].astype(I32)
        pltpu.sync_copy(head_v, head_s)
        sort_tiles_body(
            lambda k: head_s[0, k],
            lambda k: head_s[1, k],
            lambda k: head_s[2, k],
            lambda k: raw_ref[k * SIDE : (k + 1) * SIDE, :],
            count,
            outs,
            seen,
        )

    return pl.pallas_call(
        kernel,
        in_specs=[VMEM, ANY],
        out_specs=[VMEM] * RING,
        out_shape=[pltpu.VMEM((MSG, SIDE), BF16)] * RING,
        scratch_shapes=[pltpu.SMEM((OCC,), I32), pltpu.VMEM((8, SIDE), I32), pltpu.SMEM((8, SIDE), I32)],
        compiler_params=params(8),
        name="sort_far",
    )(kept(raw), after)


def turn_kernel(after, *refs):
    ins, outs = [refs[STEPS.index(d)] for d in range(RING)], refs[RING:]
    lanes = lax.broadcasted_iota(I32, (HEAD, SIDE), 1)
    heads = [r[SLOTS * SIDE :, :].astype(F32) for r in ins]
    for db in range(RING):
        head = jnp.zeros((HEAD, SIDE), F32)
        for da in range(RING):
            outs[db][da * CAP * SIDE : (da + 1) * CAP * SIDE, :] = ins[da][db * CAP * SIDE : (db + 1) * CAP * SIDE, :]
            turned = pltpu.roll(heads[da], ((da - db) * CAP) % SIDE, 1)
            head = jnp.where((lanes >= da * CAP) & (lanes < (da + 1) * CAP), turned, head)
        outs[db][SLOTS * SIDE :, :] = head.astype(BF16)


def turn(parts, after):
    return pl.pallas_call(
        turn_kernel,
        in_specs=[ANY] + [VMEM] * RING,
        out_specs=[VMEM] * RING,
        out_shape=[pltpu.VMEM((MSG, SIDE), BF16)] * RING,
        compiler_params=params(8),
        name="turn",
    )(after, *[kept(v) for v in parts])


def order(da, db):
    ahead = jnp.where(db >= 2, 2 + db, 8 + db)
    behind = jnp.where(db >= 2, 8 + db, 6 + db)
    return jnp.where(da == 0, 12 + db, jnp.where(da == 2, db, jnp.where(da == 1, ahead, behind)))


def message_places(pieces):
    return [(piece, m * MSG) for piece in pieces for m in range(piece.shape[0] // MSG)]


def group(pieces, info_v, info_s, packed):
    first, a, b = place()
    messages = message_places(pieces)
    n = len(messages) * SLOTS
    lanes = lax.broadcasted_iota(I32, (8, SIDE), 1)
    head = jnp.zeros((8, SIDE), F32)
    for i, (piece, at) in enumerate(messages):
        at += SLOTS * SIDE
        one = piece[at : at + HEAD, :].astype(F32)[0:8]
        here = (lanes >= i * SLOTS) & (lanes < (i + 1) * SLOTS)
        head = jnp.where(here, pltpu.roll(one, i * SLOTS, 1) if i else one, head)
    occ = jnp.broadcast_to(head[0:1], (8, SIDE)).astype(I32) - 1
    loc = jnp.broadcast_to(head[1:2], (8, SIDE)).astype(I32)
    da, db = relative(occ, first, a, b)
    block = jnp.where(occ >= 0, order(da, db), DUMMY)
    rows = lax.broadcasted_iota(I32, (SIDE, SIDE), 0)
    cols = lax.broadcasted_iota(I32, (SIDE, SIDE), 1)
    hot = (rows == jnp.broadcast_to(block[0:1], (SIDE, SIDE))) & (rows < OCC)
    hot = jnp.where(hot, 1.0, 0.0)
    count = jnp.broadcast_to(jnp.sum(hot, axis=1, keepdims=True), (SIDE, SIDE)).astype(I32)
    padded = (((count + 1) >> 1) << 1).astype(F32)
    below = jnp.where(cols < rows, 1.0, 0.0).astype(BF16)
    above = jnp.where(rows < cols, 1.0, 0.0).astype(BF16)
    start = jnp.dot(below, padded.astype(BF16), preferred_element_type=F32)
    rank = jnp.dot(hot.astype(BF16), above, preferred_element_type=F32)
    spot = jnp.broadcast_to(jnp.sum(hot * (start + rank), axis=0, keepdims=True), (8, SIDE)).astype(I32)
    spot = jnp.where(occ >= 0, spot, n + OCC)
    rows8 = lax.broadcasted_iota(I32, (8, SIDE), 0)
    info_v[0:8, :] = jnp.where(rows8 == 0, spot, jnp.where(rows8 == 1, loc, block))
    start = start.astype(I32)
    info_v[8:INFO, :] = jnp.where(cols == 0, start, start + count)[0 : INFO - 8, :]
    pltpu.sync_copy(info_v, info_s)
    for i in range(OCC):
        free = pl.multiple_of(info_s[8 + i, 1] * SIDE, SIDE)
        packed[pl.ds(free, SIDE), :] = jnp.zeros((SIDE, SIDE), BF16)
    for i in range(n):
        to = pl.multiple_of(info_s[0, i] * SIDE, SIDE)
        piece, at = messages[i // SLOTS]
        at += i % SLOTS * SIDE
        packed[pl.ds(to, SIDE), :] = piece[at : at + SIDE, :]


def read_lists(n, info_s, loc_s, block_s):
    for i in range(OCC):
        loc_s[info_s[8 + i, 1]] = 0
    for i in range(n):
        to = info_s[0, i]
        loc_s[to] = info_s[1, i]
        block_s[to] = info_s[2, i]


def multiply(blocks, info_s, loc_s, block_s, packed, ints, total):
    begin = info_s[8 + blocks[0], 0] >> 1
    end = info_s[8 + blocks[1], 0] >> 1

    def body(i, carry):
        for u in range(UNROLL):
            pair = begin + i * UNROLL + u
            k = jnp.minimum(pair, end - 1) * 2
            block = jnp.where(pair < end, block_s[k], DUMMY)
            at = pl.multiple_of(block * SIDE, SIDE)
            tiles = [packed[pl.ds(pl.multiple_of((k + j) * SIDE, SIDE), SIDE), :] for j in range(2)]
            rows = [ints[pl.ds(pl.multiple_of(loc_s[k + j] * SIDE, SIDE), SIDE), :] for j in range(2)]
            total[pl.ds(at, SIDE), :] += jnp.dot(
                jnp.concatenate(tiles, axis=1), jnp.concatenate(rows, axis=0), preferred_element_type=F32
            )
        return carry

    lax.fori_loop(0, (end - begin + UNROLL - 1) // UNROLL, body, 0)


def spots(n):
    return n + OCC + 2


def list_scratch(n):
    return [pltpu.SMEM((INFO, SIDE), I32), pltpu.SMEM((spots(n),), I32), pltpu.SMEM((spots(n),), I32)]


def cost(flops):
    return pl.CostEstimate(flops=flops, bytes_accessed=2**12, transcendentals=0)


def accumulate(total, ints, pieces):
    many = len(pieces)
    n = len(message_places(pieces)) * SLOTS
    old = [] if total is None else [total]

    def kernel(*refs):
        refs = refs[len(old) :]
        ints_ref, piece_refs, acc = refs[0], refs[1 : 1 + many], refs[1 + many]
        packed, info_v, info_s, loc_s, block_s = refs[2 + many :]
        if not old:
            acc[...] = jnp.zeros_like(acc)
        group(piece_refs, info_v, info_s, packed)
        read_lists(n, info_s, loc_s, block_s)
        multiply((0, OCC), info_s, loc_s, block_s, packed, ints_ref, acc)

    return pl.pallas_call(
        kernel,
        in_specs=[VMEM] * (len(old) + 1 + many),
        out_specs=VMEM,
        out_shape=pltpu.VMEM(((OCC + 1) * SIDE, ints.shape[1]), F32),
        scratch_shapes=[pltpu.VMEM((spots(n) * SIDE, SIDE), BF16), pltpu.VMEM((INFO, SIDE), I32)] + list_scratch(n),
        input_output_aliases={0: 0} if old else {},
        compiler_params=params(14),
        cost_estimate=cost(2**20),
        name="accumulate",
    )(*[kept(v) for v in old], kept(ints), *[kept(v) for v in pieces])


def finish(total, ints, late, blocks, outs, flops):
    new = late[1].dtype == BF16
    n = len(message_places(late)) * SLOTS if new else late[0].shape[0] // SIDE - OCC - 2
    width = ints.shape[1]
    given = [pltpu.VMEM((spots(n) * SIDE, SIDE), BF16), pltpu.VMEM((INFO, SIDE), I32)] if new else []

    def kernel(total_in, ints_ref, *refs):
        late_refs, acc, out_refs, rest = refs[: len(late)], refs[len(late)], refs[len(late) + 1 :][: len(outs)], refs[len(late) + 1 + len(outs) :]
        if new:
            packed, info_v, info_s, loc_s, block_s = rest
            group(late_refs, info_v, info_s, packed)
        else:
            packed, info_v = late_refs
            info_s, loc_s, block_s = rest
            pltpu.sync_copy(info_v, info_s)
        read_lists(n, info_s, loc_s, block_s)
        multiply(blocks, info_s, loc_s, block_s, packed, ints_ref, acc)
        for ref, (start, many) in zip(out_refs, outs):
            ref[...] = acc[start * SIDE : (start + many) * SIDE, :].astype(BF16)

    total, *results = pl.pallas_call(
        kernel,
        in_specs=[VMEM] * (2 + len(late)),
        out_specs=[VMEM] * (1 + len(outs) + len(given)),
        out_shape=[pltpu.VMEM(total.shape, F32)] + [pltpu.VMEM((many * SIDE, width), BF16) for _, many in outs] + given,
        scratch_shapes=list_scratch(n),
        input_output_aliases={0: 0},
        compiler_params=params(8),
        cost_estimate=cost(flops),
        name="finish",
    )(kept(total), kept(ints), *[kept(v) for v in late])
    return total, results[: len(outs)], results[len(outs) :] if new else late


def fold(total, others, outs, dtype, space):
    width = total.shape[1]

    def kernel(total_ref, *refs):
        for (start, many, terms), out in zip(outs, refs[len(others) :]):
            value = total_ref[start * SIDE : (start + many) * SIDE, :]
            for which, at in terms:
                value = value + refs[which][at * SIDE : (at + many) * SIDE, :].astype(F32)
            out[...] = value.astype(dtype)

    return pl.pallas_call(
        kernel,
        in_specs=[VMEM] * (1 + len(others)),
        out_specs=[VMEM] * len(outs),
        out_shape=[space((many * SIDE, width), dtype) for _, many, _ in outs],
        compiler_params=params(8),
        cost_estimate=cost(2**20),
        name="fold",
    )(kept(total), *[kept(v) for v in others])


def first_steps(parts):
    return [send_first(parts[d], d) if d else parts[d] for d in STEPS]


def second_steps(parts):
    return [send_second(parts[d], d) if d else parts[d] for d in STEPS]


def join(parts, after):
    sizes = [v.shape[0] for v in parts]

    def kernel(after_ref, *refs):
        at = 0
        for ref, size in zip(refs, sizes):
            refs[-1][at : at + size, :] = ref[...]
            at += size

    return pl.pallas_call(
        kernel,
        in_specs=[ANY] + [VMEM] * len(parts),
        out_specs=VMEM,
        out_shape=pltpu.VMEM((sum(sizes), SIDE), BF16),
        compiler_params=params(8),
        cost_estimate=cost(2**20),
        name="join",
    )(after, *[kept(v) for v in parts])


def hold(parts, after):
    def kernel(after_ref, *refs):
        for src, dst in zip(refs, refs[len(parts) :]):
            dst[...] = src[...]

    return pl.pallas_call(
        kernel,
        in_specs=[ANY] + [VMEM] * len(parts),
        out_specs=[VMEM] * len(parts),
        out_shape=[pltpu.VMEM(v.shape, BF16) for v in parts],
        compiler_params=params(8),
        cost_estimate=cost(2**20),
        name="hold",
    )(after, *[kept(v) for v in parts])


def load(ints):
    def kernel(src, dst, sem):
        copy = pltpu.make_async_copy(src, dst, sem)
        copy.start()
        copy.wait()

    return pl.pallas_call(
        kernel,
        in_specs=[HBM],
        out_specs=VMEM,
        out_shape=pltpu.VMEM(ints.shape, ints.dtype),
        scratch_shapes=[pltpu.SemaphoreType.DMA],
        compiler_params=params(8),
        cost_estimate=cost(2**20),
        name="load",
    )(in_hbm(ints))


def per_device(amp_tiles, owner_col, local_pair, occ_pair, integrals):
    *parts, raw = sort_own(owner_col[:, 0], local_pair, occ_pair, amp_tiles)
    far_raw = send_y(raw, 2)
    ints = load(integrals)
    turned = turn(first_steps(parts), ints)
    near = second_steps(turned)
    own = jnp.concatenate(near, axis=0)
    up, down = send_y(own, 1), send_y(own, -1)
    far_parts = sort_far(far_raw, turned[0])
    far_turned = turn(first_steps(far_parts), own)
    far = second_steps(far_turned)
    total = accumulate(None, ints, [own] + [send_core(v) for v in near])
    far_other = [send_core(v) for v in [join(far[:1], total)] + far[1:]]
    total = accumulate(total, ints, far + far_other)
    up, down, total = lax.optimization_barrier((up, down, total))
    late = [send_core(up), send_core(down)]
    total = accumulate(total, ints, [up, down])

    total, (two_ahead, two_behind), late = finish(total, ints, late, (0, 4), [(0, 2), (2, 2)], 2**31)
    from_behind, from_ahead = send_first(two_ahead, 1), send_first(two_behind, -1)
    total, (ahead, behind), late = finish(total, ints, late, (4, 8), [(4, 2), (6, 2)], 2**31)
    got = [send_first(behind, -1), send_first(ahead, 1)]
    total, _, late = finish(total, ints, late, (8, 12), [], 2**31)
    ahead, behind = fold(total, [from_behind, from_ahead], [(8, 2, [(0, 0)]), (10, 2, [(1, 0)])], BF16, pltpu.VMEM)
    got += [send_first(ahead, 1), send_first(behind, -1)]
    total, _, late = finish(total, ints, late, (12, 16), [], 2**31)
    outs = [(13, 1, [(0, 1), (2, 1)]), (14, 1, [(1, 0), (3, 0)]), (15, 1, [(1, 1), (3, 1)])]
    rest = fold(total, got, outs, BF16, pltpu.VMEM)
    last = [got[0], got[2]] + [send_second(rest[d - 1], d) for d in (2, 1, 3)]
    return fold(total, last, [(12, 1, [(i, 0) for i in range(5)])], BF16, jax.ShapeDtypeStruct)[0]


def solution(mesh):
    return jax.shard_map(
        per_device,
        mesh=mesh,
        in_specs=(
            P(("row", "col"), None, None),
            P(("row", "col"), None),
            P(("row", "col")),
            P(("row", "col")),
            P("col", "row"),
        ),
        out_specs=P("col", "row"),
        check_vma=False,
    )
```

```python
import jax
import jax.numpy as jnp
from jax import lax
from jax.experimental import pallas as pl
from jax.experimental.pallas import tpu as pltpu
from jax.sharding import PartitionSpec as P

SIDE = 128
CAP = 2
RING = 4
SLOTS = RING * CAP
HEAD = 16
MSG = SLOTS * SIDE + HEAD
PIECE = RING * MSG
OCC = RING * RING
STEPS = (0, 2, 1, 3)
DUMMY = OCC
UNROLL = 4
INFO = 32

VMEM = pl.BlockSpec(memory_space=pltpu.VMEM)
SMEM = pl.BlockSpec(memory_space=pltpu.SMEM)
ANY = pl.BlockSpec(memory_space=pl.ANY)
HBM = pl.BlockSpec(memory_space=pltpu.HBM)
F32, BF16, I32 = jnp.float32, jnp.bfloat16, jnp.int32


def row_perm(step):
    return [(r, (r + 2 * step) % (2 * RING)) for r in range(2 * RING)]


CORE_PERM = [(r, r ^ 1) for r in range(2 * RING)]


def plane_perm(step, second):
    pairs = []
    for r in range(2 * RING):
        for x in range(RING):
            for z in range(RING):
                along_x = (r % 2 == 0) != second
                nx, nz = ((x + step) % RING, z) if along_x else (x, (z + step) % RING)
                pairs.append((r * OCC + x * RING + z, r * OCC + nx * RING + nz))
    return pairs


def send_first(v, step):
    return lax.ppermute(v, ("row", "col"), plane_perm(step, False))


def send_second(v, step):
    return lax.ppermute(v, ("row", "col"), plane_perm(step, True))


def send_y(v, step):
    return lax.ppermute(v, "row", row_perm(step))


def send_core(v):
    return lax.ppermute(v, "row", CORE_PERM)


def place():
    core = lax.rem(lax.axis_index("row"), 2)
    col = lax.axis_index("col")
    x, z = col // RING, lax.rem(col, RING)
    first = core == 0
    return first, jnp.where(first, x, z), jnp.where(first, z, x)


def relative(index, first, a, b):
    x, z = index >> 2, index & 3
    return (jnp.where(first, x, z) - a) & 3, (jnp.where(first, z, x) - b) & 3


def params(mib):
    return pltpu.CompilerParams(vmem_limit_bytes=mib * 2**20)


def kept(v):
    return pltpu.with_memory_space_constraint(v, pltpu.VMEM)


def in_hbm(v):
    return pltpu.with_memory_space_constraint(v, pltpu.HBM)


def header(lines):
    rows = lax.broadcasted_iota(I32, (HEAD, SIDE), 0)
    head = jnp.zeros((HEAD, SIDE), F32)
    for i, line in enumerate(lines):
        head = jnp.where(rows == i, jnp.broadcast_to(line, (HEAD, SIDE)), head)
    return head.astype(BF16)


def sort_tiles_body(owner_of, loc_at, occ_at, tile_at, count, outs, seen):
    first, a, b = place()
    for o in range(OCC):
        seen[o] = 0
    rows = lax.broadcasted_iota(I32, (8, SIDE), 0)
    lanes = lax.broadcasted_iota(I32, (8, SIDE), 1)
    occ_of = jnp.zeros((8, SIDE), F32)
    loc_of = jnp.zeros((8, SIDE), F32)
    for k in range(count):
        owner = owner_of(k)
        rank = seen[owner]
        seen[owner] = rank + 1
        da, db = relative(owner, first, a, b)
        slot = db * CAP + rank
        here = (rows == da) & (lanes == slot)
        occ_of = jnp.where(here, (occ_at(k) + 1).astype(F32), occ_of)
        loc_of = jnp.where(here, loc_at(k).astype(F32), loc_of)
        at = pl.ds(pl.multiple_of(slot * SIDE, SIDE), SIDE)
        for d in range(RING):

            @pl.when(da == d)
            def _(d=d, k=k, at=at):
                outs[d][at, :] = tile_at(k)

    for d in range(RING):
        outs[d][SLOTS * SIDE :, :] = header([occ_of[d : d + 1], loc_of[d : d + 1]])


def sort_own(owner, loc, occ, tiles):
    count = tiles.shape[0]

    def kernel(owner_hbm, loc_hbm, occ_hbm, tiles_hbm, *refs):
        outs, raw, seen = refs[:RING], refs[RING], refs[RING + 1]
        owner_ref, loc_ref, occ_ref, sems = refs[RING + 2 :]
        pairs = [(owner_hbm, owner_ref), (loc_hbm, loc_ref), (occ_hbm, occ_ref)]
        pairs += [(tiles_hbm.at[k], raw.at[pl.ds(k * SIDE, SIDE), :]) for k in range(count)]
        copies = [pltpu.make_async_copy(src, dst, sems.at[i]) for i, (src, dst) in enumerate(pairs)]
        for copy in copies:
            copy.start()
        for copy in copies:
            copy.wait()
        sort_tiles_body(
            lambda k: owner_ref[k],
            lambda k: loc_ref[k],
            lambda k: occ_ref[k],
            lambda k: raw[k * SIDE : (k + 1) * SIDE, :],
            count,
            outs,
            seen,
        )
        lanes = lax.broadcasted_iota(I32, (8, SIDE), 1)
        rows = []
        for ref in (owner_ref, loc_ref, occ_ref):
            row = jnp.zeros((8, SIDE), F32)
            for k in range(count):
                row = jnp.where(lanes == k, ref[k].astype(F32), row)
            rows.append(row[0:1])
        raw[count * SIDE :, :] = header(rows)

    return pl.pallas_call(
        kernel,
        in_specs=[HBM] * 4,
        out_specs=[VMEM] * (RING + 1),
        out_shape=[pltpu.VMEM((MSG, SIDE), BF16)] * RING + [pltpu.VMEM((count * SIDE + HEAD, SIDE), BF16)],
        scratch_shapes=[pltpu.SMEM((OCC,), I32)]
        + [pltpu.SMEM((count,), I32)] * 3
        + [pltpu.SemaphoreType.DMA((3 + count,))],
        compiler_params=params(8),
        name="sort_own",
    )(*[in_hbm(v) for v in (owner, loc, occ, tiles)])


def sort_far(raw, after):
    count = (raw.shape[0] - HEAD) // SIDE

    def kernel(raw_ref, after_ref, *refs):
        outs, seen, head_v, head_s = refs[:RING], refs[RING], refs[RING + 1], refs[RING + 2]
        head_v[...] = raw_ref[count * SIDE :, :].astype(F32)[0:8].astype(I32)
        pltpu.sync_copy(head_v, head_s)
        sort_tiles_body(
            lambda k: head_s[0, k],
            lambda k: head_s[1, k],
            lambda k: head_s[2, k],
            lambda k: raw_ref[k * SIDE : (k + 1) * SIDE, :],
            count,
            outs,
            seen,
        )

    return pl.pallas_call(
        kernel,
        in_specs=[VMEM, ANY],
        out_specs=[VMEM] * RING,
        out_shape=[pltpu.VMEM((MSG, SIDE), BF16)] * RING,
        scratch_shapes=[pltpu.SMEM((OCC,), I32), pltpu.VMEM((8, SIDE), I32), pltpu.SMEM((8, SIDE), I32)],
        compiler_params=params(8),
        name="sort_far",
    )(kept(raw), after)


def turn_kernel(after, *refs):
    ins, outs = [refs[STEPS.index(d)] for d in range(RING)], refs[RING:]
    lanes = lax.broadcasted_iota(I32, (HEAD, SIDE), 1)
    heads = [r[SLOTS * SIDE :, :].astype(F32) for r in ins]
    for db in range(RING):
        head = jnp.zeros((HEAD, SIDE), F32)
        for da in range(RING):
            outs[db][da * CAP * SIDE : (da + 1) * CAP * SIDE, :] = ins[da][db * CAP * SIDE : (db + 1) * CAP * SIDE, :]
            turned = pltpu.roll(heads[da], ((da - db) * CAP) % SIDE, 1)
            head = jnp.where((lanes >= da * CAP) & (lanes < (da + 1) * CAP), turned, head)
        outs[db][SLOTS * SIDE :, :] = head.astype(BF16)


def turn(parts, after):
    return pl.pallas_call(
        turn_kernel,
        in_specs=[ANY] + [VMEM] * RING,
        out_specs=[VMEM] * RING,
        out_shape=[pltpu.VMEM((MSG, SIDE), BF16)] * RING,
        compiler_params=params(8),
        name="turn",
    )(after, *[kept(v) for v in parts])


def order(da, db):
    ahead = jnp.where(db >= 2, 2 + db, 8 + db)
    behind = jnp.where(db >= 2, 8 + db, 6 + db)
    return jnp.where(da == 0, 12 + db, jnp.where(da == 2, db, jnp.where(da == 1, ahead, behind)))


def message_places(pieces):
    return [(piece, m * MSG) for piece in pieces for m in range(piece.shape[0] // MSG)]


def group(pieces, info_v, info_s, packed):
    first, a, b = place()
    messages = message_places(pieces)
    n = len(messages) * SLOTS
    lanes = lax.broadcasted_iota(I32, (8, SIDE), 1)
    head = jnp.zeros((8, SIDE), F32)
    for i, (piece, at) in enumerate(messages):
        at += SLOTS * SIDE
        one = piece[at : at + HEAD, :].astype(F32)[0:8]
        here = (lanes >= i * SLOTS) & (lanes < (i + 1) * SLOTS)
        head = jnp.where(here, pltpu.roll(one, i * SLOTS, 1) if i else one, head)
    occ = jnp.broadcast_to(head[0:1], (8, SIDE)).astype(I32) - 1
    loc = jnp.broadcast_to(head[1:2], (8, SIDE)).astype(I32)
    da, db = relative(occ, first, a, b)
    block = jnp.where(occ >= 0, order(da, db), DUMMY)
    rows = lax.broadcasted_iota(I32, (SIDE, SIDE), 0)
    cols = lax.broadcasted_iota(I32, (SIDE, SIDE), 1)
    hot = (rows == jnp.broadcast_to(block[0:1], (SIDE, SIDE))) & (rows < OCC)
    hot = jnp.where(hot, 1.0, 0.0)
    count = jnp.broadcast_to(jnp.sum(hot, axis=1, keepdims=True), (SIDE, SIDE)).astype(I32)
    padded = (((count + 1) >> 1) << 1).astype(F32)
    below = jnp.where(cols < rows, 1.0, 0.0).astype(BF16)
    above = jnp.where(rows < cols, 1.0, 0.0).astype(BF16)
    start = jnp.dot(below, padded.astype(BF16), preferred_element_type=F32)
    rank = jnp.dot(hot.astype(BF16), above, preferred_element_type=F32)
    spot = jnp.broadcast_to(jnp.sum(hot * (start + rank), axis=0, keepdims=True), (8, SIDE)).astype(I32)
    spot = jnp.where(occ >= 0, spot, n + OCC)
    rows8 = lax.broadcasted_iota(I32, (8, SIDE), 0)
    info_v[0:8, :] = jnp.where(rows8 == 0, spot, jnp.where(rows8 == 1, loc, block))
    start = start.astype(I32)
    info_v[8:INFO, :] = jnp.where(cols == 0, start, start + count)[0 : INFO - 8, :]
    pltpu.sync_copy(info_v, info_s)
    for i in range(OCC):
        free = pl.multiple_of(info_s[8 + i, 1] * SIDE, SIDE)
        packed[pl.ds(free, SIDE), :] = jnp.zeros((SIDE, SIDE), BF16)
    for i in range(n):
        to = pl.multiple_of(info_s[0, i] * SIDE, SIDE)
        piece, at = messages[i // SLOTS]
        at += i % SLOTS * SIDE
        packed[pl.ds(to, SIDE), :] = piece[at : at + SIDE, :]


def read_lists(n, info_s, loc_s, block_s):
    for i in range(OCC):
        loc_s[info_s[8 + i, 1]] = 0
    for i in range(n):
        to = info_s[0, i]
        loc_s[to] = info_s[1, i]
        block_s[to] = info_s[2, i]


def multiply(blocks, info_s, loc_s, block_s, packed, ints, total):
    begin = info_s[8 + blocks[0], 0] >> 1
    end = info_s[8 + blocks[1], 0] >> 1

    def body(i, carry):
        for u in range(UNROLL):
            pair = begin + i * UNROLL + u
            k = jnp.minimum(pair, end - 1) * 2
            block = jnp.where(pair < end, block_s[k], DUMMY)
            at = pl.multiple_of(block * SIDE, SIDE)
            tiles = [packed[pl.ds(pl.multiple_of((k + j) * SIDE, SIDE), SIDE), :] for j in range(2)]
            rows = [ints[pl.ds(pl.multiple_of(loc_s[k + j] * SIDE, SIDE), SIDE), :] for j in range(2)]
            total[pl.ds(at, SIDE), :] += jnp.dot(
                jnp.concatenate(tiles, axis=1), jnp.concatenate(rows, axis=0), preferred_element_type=F32
            )
        return carry

    lax.fori_loop(0, (end - begin + UNROLL - 1) // UNROLL, body, 0)


def spots(n):
    return n + OCC + 2


def list_scratch(n):
    return [pltpu.SMEM((INFO, SIDE), I32), pltpu.SMEM((spots(n),), I32), pltpu.SMEM((spots(n),), I32)]


def cost(flops):
    return pl.CostEstimate(flops=flops, bytes_accessed=2**12, transcendentals=0)


def accumulate(total, ints, pieces):
    many = len(pieces)
    n = len(message_places(pieces)) * SLOTS
    old = [] if total is None else [total]

    def kernel(*refs):
        refs = refs[len(old) :]
        ints_ref, piece_refs, acc = refs[0], refs[1 : 1 + many], refs[1 + many]
        packed, info_v, info_s, loc_s, block_s = refs[2 + many :]
        if not old:
            acc[...] = jnp.zeros_like(acc)
        group(piece_refs, info_v, info_s, packed)
        read_lists(n, info_s, loc_s, block_s)
        multiply((0, OCC), info_s, loc_s, block_s, packed, ints_ref, acc)

    return pl.pallas_call(
        kernel,
        in_specs=[VMEM] * (len(old) + 1 + many),
        out_specs=VMEM,
        out_shape=pltpu.VMEM(((OCC + 1) * SIDE, ints.shape[1]), F32),
        scratch_shapes=[pltpu.VMEM((spots(n) * SIDE, SIDE), BF16), pltpu.VMEM((INFO, SIDE), I32)] + list_scratch(n),
        input_output_aliases={0: 0} if old else {},
        compiler_params=params(14),
        cost_estimate=cost(2**20),
        name="accumulate",
    )(*[kept(v) for v in old], kept(ints), *[kept(v) for v in pieces])


def finish(total, ints, late, blocks, outs, flops):
    new = late[1].dtype == BF16
    n = len(message_places(late)) * SLOTS if new else late[0].shape[0] // SIDE - OCC - 2
    width = ints.shape[1]
    given = [pltpu.VMEM((spots(n) * SIDE, SIDE), BF16), pltpu.VMEM((INFO, SIDE), I32)] if new else []

    def kernel(total_in, ints_ref, *refs):
        late_refs, acc, out_refs, rest = refs[: len(late)], refs[len(late)], refs[len(late) + 1 :][: len(outs)], refs[len(late) + 1 + len(outs) :]
        if new:
            packed, info_v, info_s, loc_s, block_s = rest
            group(late_refs, info_v, info_s, packed)
        else:
            packed, info_v = late_refs
            info_s, loc_s, block_s = rest
            pltpu.sync_copy(info_v, info_s)
        read_lists(n, info_s, loc_s, block_s)
        multiply(blocks, info_s, loc_s, block_s, packed, ints_ref, acc)
        for ref, (start, many) in zip(out_refs, outs):
            ref[...] = acc[start * SIDE : (start + many) * SIDE, :].astype(BF16)

    total, *results = pl.pallas_call(
        kernel,
        in_specs=[VMEM] * (2 + len(late)),
        out_specs=[VMEM] * (1 + len(outs) + len(given)),
        out_shape=[pltpu.VMEM(total.shape, F32)] + [pltpu.VMEM((many * SIDE, width), BF16) for _, many in outs] + given,
        scratch_shapes=list_scratch(n),
        input_output_aliases={0: 0},
        compiler_params=params(8),
        cost_estimate=cost(flops),
        name="finish",
    )(kept(total), kept(ints), *[kept(v) for v in late])
    return total, results[: len(outs)], results[len(outs) :] if new else late


def fold(total, others, outs, dtype, space):
    width = total.shape[1]

    def kernel(total_ref, *refs):
        for (start, many, terms), out in zip(outs, refs[len(others) :]):
            value = total_ref[start * SIDE : (start + many) * SIDE, :]
            for which, at in terms:
                value = value + refs[which][at * SIDE : (at + many) * SIDE, :].astype(F32)
            out[...] = value.astype(dtype)

    return pl.pallas_call(
        kernel,
        in_specs=[VMEM] * (1 + len(others)),
        out_specs=[VMEM] * len(outs),
        out_shape=[space((many * SIDE, width), dtype) for _, many, _ in outs],
        compiler_params=params(8),
        cost_estimate=cost(2**20),
        name="fold",
    )(kept(total), *[kept(v) for v in others])


def first_steps(parts):
    return [send_first(parts[d], d) if d else parts[d] for d in STEPS]


def second_steps(parts):
    return [send_second(parts[d], d) if d else parts[d] for d in STEPS]


def join(parts, after):
    sizes = [v.shape[0] for v in parts]

    def kernel(after_ref, *refs):
        at = 0
        for ref, size in zip(refs, sizes):
            refs[-1][at : at + size, :] = ref[...]
            at += size

    return pl.pallas_call(
        kernel,
        in_specs=[ANY] + [VMEM] * len(parts),
        out_specs=VMEM,
        out_shape=pltpu.VMEM((sum(sizes), SIDE), BF16),
        compiler_params=params(8),
        cost_estimate=cost(2**20),
        name="join",
    )(after, *[kept(v) for v in parts])


def hold(parts, after):
    def kernel(after_ref, *refs):
        for src, dst in zip(refs, refs[len(parts) :]):
            dst[...] = src[...]

    return pl.pallas_call(
        kernel,
        in_specs=[ANY] + [VMEM] * len(parts),
        out_specs=[VMEM] * len(parts),
        out_shape=[pltpu.VMEM(v.shape, BF16) for v in parts],
        compiler_params=params(8),
        cost_estimate=cost(2**20),
        name="hold",
    )(after, *[kept(v) for v in parts])


def load(ints):
    def kernel(src, dst, sem):
        copy = pltpu.make_async_copy(src, dst, sem)
        copy.start()
        copy.wait()

    return pl.pallas_call(
        kernel,
        in_specs=[HBM],
        out_specs=VMEM,
        out_shape=pltpu.VMEM(ints.shape, ints.dtype),
        scratch_shapes=[pltpu.SemaphoreType.DMA],
        compiler_params=params(8),
        cost_estimate=cost(2**20),
        name="load",
    )(in_hbm(ints))


def per_device(amp_tiles, owner_col, local_pair, occ_pair, integrals):
    *parts, raw = sort_own(owner_col[:, 0], local_pair, occ_pair, amp_tiles)
    far_raw = send_y(raw, 2)
    ints = load(integrals)
    turned = turn(first_steps(parts), ints)
    near = second_steps(turned)
    own = jnp.concatenate(near, axis=0)
    up, down = send_y(own, 1), send_y(own, -1)
    far_parts = sort_far(far_raw, turned[0])
    far_turned = turn(first_steps(far_parts), own)
    far = second_steps(far_turned)
    total = accumulate(None, ints, [own] + [send_core(v) for v in near])
    far_other = [send_core(v) for v in [join(far[:1], total)] + far[1:]]
    total, _, far = finish(total, ints, far + far_other, (0, 12), [], 2**20)
    up, down, total = lax.optimization_barrier((up, down, total))
    late = [send_core(up), send_core(down)]
    total, _, middle = finish(total, ints, [up, down], (0, 12), [], 2**20)

    total, (two_ahead, two_behind), late = finish(total, ints, late, (0, 4), [(0, 2), (2, 2)], 2**31)
    from_behind, from_ahead = send_first(two_ahead, 1), send_first(two_behind, -1)
    total, (ahead, behind), late = finish(total, ints, late, (4, 8), [(4, 2), (6, 2)], 2**31)
    got = [send_first(behind, -1), send_first(ahead, 1)]
    total, _, late = finish(total, ints, late, (8, 12), [], 2**31)
    ahead, behind = fold(total, [from_behind, from_ahead], [(8, 2, [(0, 0)]), (10, 2, [(1, 0)])], BF16, pltpu.VMEM)
    got += [send_first(ahead, 1), send_first(behind, -1)]
    for packed in (far, middle, late):
        total, _, _ = finish(total, ints, packed, (12, 16), [], 2**31)
    outs = [(13, 1, [(0, 1), (2, 1)]), (14, 1, [(1, 0), (3, 0)]), (15, 1, [(1, 1), (3, 1)])]
    rest = fold(total, got, outs, BF16, pltpu.VMEM)
    last = [got[0], got[2]] + [send_second(rest[d - 1], d) for d in (2, 1, 3)]
    return fold(total, last, [(12, 1, [(i, 0) for i in range(5)])], BF16, jax.ShapeDtypeStruct)[0]


def solution(mesh):
    return jax.shard_map(
        per_device,
        mesh=mesh,
        in_specs=(
            P(("row", "col"), None, None),
            P(("row", "col"), None),
            P(("row", "col")),
            P(("row", "col")),
            P("col", "row"),
        ),
        out_specs=P("col", "row"),
        check_vma=False,
    )
```
